32 devices in a mesh: gx: 4 (over y, x), gy: 8 (over z, core).
Axes of the slice: x: 2, y: 2, z: 4, core: 2. Of those that a mesh axis runs over, the one named last changes fastest.
Arguments:
- right_side: float32 [3, 16, 64, 128], P(None, 'gx', 'gy'), may hold values from -8 to 8
- stiffness: float32 [16, 64, 128], P('gx', 'gy'), may hold values from 2.5 to 25
- panels: float32 [64, 3, 16, 64, 128], P(None, None, 'gx', 'gy'), may hold values from -0.21 to 0.21
Outputs:
- solution: float32 [3, 16, 64, 128], P(None, 'gx', 'gy')
- residual: float32 [3, 16, 64, 128], P(None, 'gx', 'gy')
- coupling: float32 [4, 8, 8, 4096], P('gx', 'gy')
The draws below stay inside these ranges and needn't reach their ends.
All inputs are finite; a program needn't handle non-finite values.
Results may differ from the reference program's by a relative error of at most 0.0003.
Values sent between devices are 32-bit elements; how exact they have to be, the bound alone decides.
A program may use at most 192 MiB of HBM per device.

```python
import math
import jax
import jax.numpy as jnp
from jax import lax

CX = 4
CY = 8
CZ = 128
PANELS = 64
SWEEPS = 4
ITERS = 2
NX = 16
NY = 64
N_GX = 4
N_GY = 8


def spread_blocks(values):
    widened = jnp.repeat(values, CX, axis=2, total_repeat_length=NX)
    return jnp.repeat(widened, CY, axis=3, total_repeat_length=NY)


def draw_panels(key, part):
    key_list = jax.random.split(jax.random.fold_in(key, 11), 9)
    block_grid = (PANELS, 3, NX // CX, NY // CY)
    panel_order = jnp.arange(PANELS, dtype=jnp.int32)
    mode_first = (panel_order % 4).astype(jnp.float32)[:, None, None, None]
    mode_second = (panel_order // 4 % 4).astype(jnp.float32)[:, None, None, None]
    mode_third = (panel_order // 16 % 4).astype(jnp.float32)[:, None, None, None]
    freq_first = spread_blocks(mode_first + jax.random.uniform(key_list[0], block_grid, jnp.float32, 0.0, 0.6))
    freq_second = spread_blocks(mode_second + jax.random.uniform(key_list[1], block_grid, jnp.float32, 0.0, 0.6))
    freq_third = spread_blocks(mode_third + jax.random.uniform(key_list[2], block_grid, jnp.float32, 0.0, 0.6))
    phase_first = spread_blocks(jax.random.uniform(key_list[3], block_grid, jnp.float32, -0.5, 0.5))
    phase_second = spread_blocks(jax.random.uniform(key_list[4], block_grid, jnp.float32, -0.5, 0.5))
    phase_third = spread_blocks(jax.random.uniform(key_list[5], block_grid, jnp.float32, -0.5, 0.5))
    full_shape = (PANELS, 3, NX, NY, CZ)
    magnitude = jnp.exp(jax.random.uniform(key_list[6], block_grid, jnp.float32, math.log(0.5), math.log(1.6)))
    rough_part = 0.15 * jax.random.truncated_normal(key_list[8], -3.0, 3.0, full_shape, jnp.float32)
    sign_values = (2 * jax.random.randint(key_list[7], block_grid, 0, 2) - 1).astype(jnp.float32)
    amplitude = spread_blocks(magnitude * sign_values)
    local_first = ((jnp.arange(NX) % CX).astype(jnp.float32) + 0.5) / CX
    local_second = ((jnp.arange(NY) % CY).astype(jnp.float32) + 0.5) / CY
    local_third = (jnp.arange(CZ).astype(jnp.float32) + 0.5) / CZ
    wave_first = jnp.cos(math.pi * (freq_first * local_first[:, None] + phase_first))
    wave_second = jnp.cos(math.pi * (freq_second * local_second[None, :] + phase_second))
    wave_third = jnp.cos(math.pi * (freq_third[..., None] * local_third + phase_third[..., None]))
    smooth_part = (amplitude * wave_first * wave_second)[..., None] * wave_third
    return (0.09 * (smooth_part + rough_part)).astype(jnp.float32)


def draw_right_side(key, part):
    key_list = jax.random.split(jax.random.fold_in(key, 23), 9)
    full_shape = (3, NX, NY, CZ)
    comp_shape = (3, 1, 1, 1)
    coord_first = ((jnp.arange(NX).astype(jnp.float32) + 0.5) / NX)[:, None, None]
    coord_second = ((jnp.arange(NY).astype(jnp.float32) + 0.5) / NY)[None, :, None]
    coord_third = (jnp.arange(CZ).astype(jnp.float32) + 0.5) / CZ
    freq_first = jax.random.uniform(key_list[0], comp_shape, jnp.float32, 0.5, 1.5)
    freq_second = jax.random.uniform(key_list[1], comp_shape, jnp.float32, 0.5, 1.5)
    freq_third = jax.random.uniform(key_list[2], comp_shape, jnp.float32, 0.5, 1.5)
    phase_first = jax.random.uniform(key_list[3], comp_shape, jnp.float32, -0.3, 0.3)
    phase_second = jax.random.uniform(key_list[4], comp_shape, jnp.float32, -0.3, 0.3)
    phase_third = jax.random.uniform(key_list[5], comp_shape, jnp.float32, -0.3, 0.3)
    wave_field = jnp.cos(math.pi * (freq_first * coord_first + phase_first))
    wave_field = wave_field * jnp.cos(math.pi * (freq_second * coord_second + phase_second))
    wave_field = wave_field * jnp.cos(math.pi * (freq_third * coord_third + phase_third))
    base_level = jax.random.uniform(key_list[6], comp_shape, jnp.float32, -0.8, 0.8)
    swing_size = jax.random.uniform(key_list[7], comp_shape, jnp.float32, 0.5, 1.0)
    rough_part = jax.random.truncated_normal(key_list[8], -6.0, 6.0, full_shape, jnp.float32)
    return (base_level + swing_size * wave_field + rough_part).astype(jnp.float32)


def block_levels(rng, extent, shards, low, top_value):
    loudness, own = 1.0, jax.random.fold_in(rng, 6)
    for dim, shards_of in shards:
        draws = jnp.exp(jax.random.uniform(jax.random.fold_in(own, dim), (shards_of,), jnp.float32, low / len(shards), top_value / len(shards)))
        loudness = loudness * jnp.repeat(draws, extent[dim] // shards_of).reshape([-1 if axis == dim else 1 for axis in range(len(extent))])
    return loudness


def setup_inputs(seed: int = 0) -> dict:
    splits = jax.random.split(jax.random.key(seed), 4)
    return {
        "right_side": draw_right_side(jax.random.fold_in(splits[3], 71), 0),
        "stiffness": jnp.clip(jnp.exp(math.log(25.0) - 2.3025851 * jax.random.uniform(splits[1], (NX, NY, CZ), jnp.float32) ** block_levels(splits[1], (NX, NY, CZ), ((0, 4), (1, 8)), -0.2, 0.2)), 2.5, 25.0),
        "panels": draw_panels(jax.random.fold_in(splits[3], 71), 0),
    }


precise = lax.Precision.HIGHEST
mixing = 0.25
damping = 0.5
neighbours = ((-1, -1), (-1, 0), (-1, 1), (0, -1), (0, 1), (1, -1), (1, 0), (1, 1))


def apply_stencil(window, stiff_block):
    paddings = [(0, 0)] * (window.ndim - 1) + [(1, 1)]
    widened = jnp.pad(window, paddings)
    along_first = widened[..., :-2, :, :] + widened[..., 1:-1, :, :] + widened[..., 2:, :, :]
    along_second = along_first[..., :, :-2, :] + along_first[..., :, 1:-1, :] + along_first[..., :, 2:, :]
    box_sum = along_second[..., :-2] + along_second[..., 1:-1] + along_second[..., 2:]
    centre = window[..., 1:-1, 1:-1, :]
    slope_first = widened[..., 2:, :, :] - widened[..., :-2, :, :]
    slope_second = widened[..., 1:-1, 2:, :] - widened[..., 1:-1, :-2, :]
    mixed_ab = slope_first[..., :, 2:, 1:-1] - slope_first[..., :, :-2, 1:-1]
    mixed_ac = slope_first[..., :, 1:-1, 2:] - slope_first[..., :, 1:-1, :-2]
    mixed_bc = slope_second[..., 2:] - slope_second[..., :-2]
    cross_terms = jnp.stack([
        mixed_ab[..., 1, :, :, :] + mixed_ac[..., 2, :, :, :],
        mixed_ab[..., 0, :, :, :] + mixed_bc[..., 2, :, :, :],
        mixed_ac[..., 0, :, :, :] + mixed_bc[..., 1, :, :, :]], axis=-4)
    return (27.0 + stiff_block) * centre - box_sum + mixing * cross_terms


def window_plan(offset, length):
    if offset == 0:
        return (0, length + 2, 1, length + 1, 0, length)
    if offset == 1:
        return (length - 1, length + 2, 2, 3, length - 1, length)
    return (0, 3, 0, 1, 0, 1)


def select_mask(plan):
    places = jnp.arange(plan[1] - plan[0])
    return ((places >= plan[2]) & (places < plan[3])).astype(jnp.float32)


def coarse_tile(padded, own_panels, stiff_block, shift_first, shift_second):
    plan_first = window_plan(shift_first, own_panels.shape[2])
    plan_second = window_plan(shift_second, own_panels.shape[3])
    window = padded[:, :, plan_first[0]:plan_first[1], plan_second[0]:plan_second[1], :]
    keep_first = select_mask(plan_first)
    keep_second = select_mask(plan_second)
    masked = window * (keep_first[:, None, None] * keep_second[None, :, None])
    imaged = apply_stencil(masked, stiff_block[plan_first[4]:plan_first[5], plan_second[4]:plan_second[5], :])
    panel_part = own_panels[:, :, plan_first[4]:plan_first[5], plan_second[4]:plan_second[5], :]
    return jnp.einsum("kabcd,labcd->kl", panel_part, imaged, precision=precise)


def jacobi(ext_residual, ext_stiff):
    inv_diag = damping / (26.0 + ext_stiff)
    correction = inv_diag * ext_residual
    for sweep_index in range(SWEEPS - 1):
        widened = jnp.pad(correction, ((0, 0), (1, 1), (1, 1), (0, 0)))
        correction = correction + inv_diag * (ext_residual - apply_stencil(widened, ext_stiff))
    return correction


def reference(right_side, stiffness, panels):
    anchor = jnp.int32(0)
    block_ids = jnp.arange(N_GX * N_GY, dtype=jnp.int32)
    panels_wide = jnp.pad(panels, ((0, 0), (0, 0), (1, 1), (1, 1), (0, 0)))
    stiff_wide = jnp.pad(stiffness, ((1, 1), (1, 1), (0, 0)))

    def block_tiles(block_index):
        block_row = block_index // N_GY
        block_column = block_index % N_GY
        padded = lax.dynamic_slice(panels_wide, (anchor, anchor, block_row * CX, block_column * CY, anchor), (PANELS, 3, CX + 2, CY + 2, CZ))
        stiff_block = lax.dynamic_slice(stiffness, (block_row * CX, block_column * CY, anchor), (CX, CY, CZ))
        own_panels = padded[:, :, 1:-1, 1:-1, :]
        diag_tile = coarse_tile(padded, own_panels, stiff_block, 0, 0)
        others = jnp.stack([coarse_tile(padded, own_panels, stiff_block, shift_first, shift_second) for shift_first, shift_second in neighbours])
        return diag_tile, others

    diag_all, coupling_all = lax.map(block_tiles, block_ids)
    diag_all = diag_all.reshape(N_GX, N_GY, PANELS, PANELS)
    coupling_all = coupling_all.reshape(N_GX, N_GY, 8, PANELS, PANELS)
    weights = damping / jnp.diagonal(diag_all, axis1=2, axis2=3)
    panels_view = panels.reshape(PANELS, 3, N_GX, CX, N_GY, CY, CZ)

    def coarse_times(vector):
        vector_wide = jnp.pad(vector, ((1, 1), (1, 1), (0, 0)))
        totals = jnp.einsum("ghkl,ghl->ghk", diag_all, vector, precision=precise)
        for place, (shift_first, shift_second) in enumerate(neighbours):
            shifted = vector_wide[1 + shift_first:1 + shift_first + N_GX, 1 + shift_second:1 + shift_second + N_GY]
            totals = totals + jnp.einsum("ghkl,ghl->ghk", coupling_all[:, :, place], shifted, precision=precise)
        return totals

    def precondition(current):
        current_view = current.reshape(3, N_GX, CX, N_GY, CY, CZ)
        restricted = jnp.einsum("kagchdz,agchdz->ghk", panels_view, current_view, precision=precise)
        first_guess = weights * restricted
        coarse_vec = first_guess + weights * (restricted - coarse_times(first_guess))
        coarse_part = jnp.einsum("kagchdz,ghk->agchdz", panels_view, coarse_vec, precision=precise).reshape(3, NX, NY, CZ)
        current_wide = jnp.pad(current, ((0, 0), (1, 1), (1, 1), (0, 0)))

        def local_block(block_index):
            block_row = block_index // N_GY
            block_column = block_index % N_GY
            ext_residual = lax.dynamic_slice(current_wide, (anchor, block_row * CX, block_column * CY, anchor), (3, CX + 2, CY + 2, CZ))
            ext_stiff = lax.dynamic_slice(stiff_wide, (block_row * CX, block_column * CY, anchor), (CX + 2, CY + 2, CZ))
            return jacobi(ext_residual, ext_stiff)

        pieces = lax.map(local_block, block_ids)

        def accumulate(counter, summed):
            block_index = jnp.asarray(counter).astype(jnp.int32)
            block_row = block_index // N_GY
            block_column = block_index % N_GY
            starts = (anchor, block_row * CX, block_column * CY, anchor)
            present = lax.dynamic_slice(summed, starts, (3, CX + 2, CY + 2, CZ))
            return lax.dynamic_update_slice(summed, present + pieces[block_index], starts)

        summed = lax.fori_loop(0, N_GX * N_GY, accumulate, jnp.zeros((3, NX + 2, NY + 2, CZ), jnp.float32))
        return summed[:, 1:-1, 1:-1, :] + coarse_part

    def operate(field_in):
        return apply_stencil(jnp.pad(field_in, ((0, 0), (1, 1), (1, 1), (0, 0))), stiffness)

    solution = jnp.zeros_like(right_side)
    residual = right_side
    precond = precondition(residual)
    direction = precond
    fit_now = jnp.sum(residual * precond)
    for iteration in range(ITERS):
        imaged = operate(direction)
        step_size = fit_now / jnp.sum(direction * imaged)
        solution = solution + step_size * direction
        residual = residual - step_size * imaged
        if iteration + 1 < ITERS:
            precond = precondition(residual)
            fit_next = jnp.sum(residual * precond)
            direction = precond + (fit_next / fit_now) * direction
            fit_now = fit_next
    coupling = coupling_all.reshape(N_GX, N_GY, 8, PANELS * PANELS)
    return (solution, residual, coupling)
```

```python
import functools

import jax
import jax.numpy as jnp
from jax import lax
from jax.experimental import pallas as pl
from jax.experimental.pallas import tpu as pltpu
from jax.sharding import PartitionSpec as P

SWEEPS = 4
MESH = pl.DeviceIdType.MESH
mixing = 0.25
damping = 0.5
neighbours = ((-1, -1), (-1, 0), (-1, 1), (0, -1), (0, 1), (1, -1), (1, 0), (1, 1))
ROUNDS = 8


def shift_z(value, step):
    axis = value.ndim - 1
    size = value.shape[axis]
    rolled = pltpu.roll(value, (-step) % size, axis)
    lane = lax.broadcasted_iota(jnp.int32, value.shape, axis)
    edge = size - 1 if step == 1 else 0
    return jnp.where(lane == edge, 0.0, rolled)


def shift_lead(value, step, axis):
    size = value.shape[axis]
    zero = jnp.zeros_like(lax.slice_in_dim(value, 0, 1, axis=axis))
    if step == 1:
        return jnp.concatenate([lax.slice_in_dim(value, 1, size, axis=axis), zero], axis=axis)
    return jnp.concatenate([zero, lax.slice_in_dim(value, 0, size - 1, axis=axis)], axis=axis)


def stencil(field, start, count):
    def planes(c, step):
        return field[c, start + step : start + step + count]

    def up(v):
        return pltpu.roll(v, 15, 1)

    def down(v):
        return pltpu.roll(v, 1, 1)

    low = [planes(c, -1) for c in range(3)]
    mid = [planes(c, 0) for c in range(3)]
    high = [planes(c, 1) for c in range(3)]
    box = []
    for c in range(3):
        along = low[c] + mid[c] + high[c]
        box.append(along + up(along) + down(along))
    dx0, dx1, dx2 = (high[c] - low[c] for c in range(3))
    dy1 = up(mid[1]) - down(mid[1])
    dz2 = shift_z(mid[2], 1) - shift_z(mid[2], -1)
    side0 = mixing * dx2
    out0 = (
        mixing * (up(dx1) - down(dx1)) - box[0] + shift_z(side0 - box[0], 1) - shift_z(side0 + box[0], -1)
    )
    side1 = mixing * (dx0 + dz2)
    out1 = up(side1) - down(side1) - box[1] - shift_z(box[1], 1) - shift_z(box[1], -1)
    side2 = mixing * (dx0 + dy1)
    out2 = shift_z(side2 - box[2], 1) - shift_z(side2 + box[2], -1) - box[2]
    return out0, out1, out2


def ring_image(edge, sx, sy):
    boxes = []
    for c in range(3):
        v = edge[c]
        if sx == 0 or sy == 0:
            v = v + shift_lead(v, 1, 0) + shift_lead(v, -1, 0)
        boxes.append(v + shift_z(v, 1) + shift_z(v, -1))
    if sx and sy:
        return [mixing * sx * sy * edge[1] - boxes[0], mixing * sx * sy * edge[0] - boxes[1], -boxes[2]]

    def along(v):
        return shift_lead(v, 1, 0) - shift_lead(v, -1, 0)

    def third(v):
        return shift_z(v, 1) - shift_z(v, -1)

    if sx:
        return [
            -mixing * sx * (along(edge[1]) + third(edge[2])) - boxes[0],
            -mixing * sx * along(edge[0]) - boxes[1],
            -mixing * sx * third(edge[0]) - boxes[2],
        ]
    return [
        -mixing * sy * along(edge[1]) - boxes[0],
        -mixing * sy * (along(edge[0]) + third(edge[2])) - boxes[1],
        -mixing * sy * third(edge[1]) - boxes[2],
    ]


def split_rows(value):
    high = value.astype(jnp.bfloat16)
    low = (value - high.astype(jnp.float32)).astype(jnp.bfloat16)
    return jnp.concatenate([high, low], axis=0)


def kernel(
    n_gx, n_gy, r_ref, s_ref, z_ref, x_out, res_out, tile_out,
    panel, far_x, far_y, far_c, image_x, send, recv, ext, ext_r, ext_inv, own_p, own_z, own_w, own_v, own_u,
    weight, coarse, dots, sums_x, sums_y,
    send_sem, recv_sem, far_send, far_recv, sx_send, sx_recv, sy_send, sy_recv,
):
    X, Y, Z = s_ref.shape
    K = panel.shape[3]
    rows = 3 * X * Y
    gx, gy = lax.axis_index("gx"), lax.axis_index("gy")

    def exists(d):
        sx, sy = neighbours[d]
        ok = jnp.bool_(True)
        if sx < 0:
            ok = gx > 0
        if sx > 0:
            ok = gx < n_gx - 1
        if sy:
            ok_y = gy > 0 if sy < 0 else gy < n_gy - 1
            ok = jnp.logical_and(ok, ok_y) if sx else ok_y
        return ok

    def peer(d):
        return (gx + neighbours[d][0], gy + neighbours[d][1])

    recv[...] = jnp.zeros_like(recv)
    ext[...] = jnp.zeros_like(ext)
    ext_r[...] = jnp.zeros_like(ext_r)
    ext_inv[...] = jnp.zeros_like(ext_inv)
    dots[...] = jnp.zeros_like(dots)
    barrier = pltpu.get_barrier_semaphore()
    count = jnp.int32(n_gx - 1 + n_gy - 1)
    for o in range(1, n_gx):
        pl.semaphore_signal(barrier, inc=1, device_id=(lax.rem(gx + o, n_gx), gy), device_id_type=MESH)
    for o in range(1, n_gy):
        pl.semaphore_signal(barrier, inc=1, device_id=(gx, lax.rem(gy + o, n_gy)), device_id_type=MESH)
    for d in (0, 2, 5, 7):
        count = count + exists(d).astype(jnp.int32)

        @pl.when(exists(d))
        def _():
            pl.semaphore_signal(barrier, inc=1, device_id=peer(d), device_id_type=MESH)

    pl.semaphore_wait(barrier, count)

    def length(d, with_stiff):
        sx, sy = neighbours[d]
        if sx and sy:
            return 8
        if sx:
            return 32 if with_stiff else 24
        return 16

    def message(turn, d):
        n = length(d, turn == 0)
        return pltpu.make_async_remote_copy(
            src_ref=send.at[turn, d, 0:n],
            dst_ref=recv.at[turn, 7 - d, 0:n],
            send_sem=send_sem.at[turn, d],
            recv_sem=recv_sem.at[turn, 7 - d],
            device_id=peer(d),
            device_id_type=MESH,
        )

    def arrival(turn, d):
        n = length(d, turn == 0)
        return pltpu.make_async_remote_copy(
            src_ref=send.at[turn, d, 0:n],
            dst_ref=recv.at[turn, d, 0:n],
            send_sem=send_sem.at[turn, d],
            recv_sem=recv_sem.at[turn, d],
            device_id=peer(d),
            device_id_type=MESH,
        )

    def launch(turn):
        for d in range(8):

            @pl.when(exists(d))
            def _():
                message(turn, d).start()

    def await_all(turn):
        for d in range(8):

            @pl.when(exists(d))
            def _():
                arrival(turn, d).wait_recv()

    def pack_own(turn, field):
        for d, (sx, sy) in enumerate(neighbours):
            px, py = (0 if sx < 0 else X - 1), (0 if sy < 0 else Y - 1)
            for c in range(3):
                if sx and sy:
                    send[turn, d, c, :] = field[c, px, py, :]
                elif sx:
                    send[turn, d, c * Y : (c + 1) * Y, :] = field[c, px]
                else:
                    for x in range(X):
                        send[turn, d, c * X + x, :] = field[c, x, py, :]

    def pack_ring(turn):
        for d, (sx, sy) in enumerate(neighbours):
            px, py = (1 if sx < 0 else X + 2), (15 if sy < 0 else 8)
            for c in range(3):
                if sx and sy:
                    send[turn, d, c, :] = ext[c, px, py, :]
                elif sx:
                    send[turn, d, c * Y : (c + 1) * Y, :] = ext[c, px, 0:Y]
                else:
                    for x in range(X):
                        send[turn, d, c * X + x, :] = ext[c, 2 + x, py, :]

    def unpack_halo(turn, target):
        for d, (sx, sy) in enumerate(neighbours):
            px, py = (1 if sx < 0 else X + 2), (15 if sy < 0 else 8)
            for c in range(3):
                if sx and sy:
                    target[c, px, py, :] = recv[turn, d, c, :]
                elif sx:
                    target[c, px, 0:Y] = recv[turn, d, c * Y : (c + 1) * Y, :]
                else:
                    for x in range(X):
                        target[c, 2 + x, py, :] = recv[turn, d, c * X + x, :]

    def add_ring(turn, target):
        for d, (sx, sy) in enumerate(neighbours):
            px, py = (0 if sx < 0 else X - 1), (0 if sy < 0 else Y - 1)
            for c in range(3):
                if sx and sy:
                    target[c, px, py, :] += recv[turn, d, c, :]
                elif sx:
                    target[c, px] += recv[turn, d, c * Y : (c + 1) * Y, :]
                else:
                    for x in range(X):
                        target[c, x, py, :] += recv[turn, d, c * X + x, :]

    pack_own(0, r_ref)
    for d, (sx, sy) in enumerate(neighbours):
        px, py = (0 if sx < 0 else X - 1), (0 if sy < 0 else Y - 1)
        if sx and sy:
            send[0, d, 3, :] = s_ref[px, py, :]
        elif sx:
            send[0, d, 3 * Y : 4 * Y, :] = s_ref[px]
        else:
            for x in range(X):
                send[0, d, 3 * X + x, :] = s_ref[x, py, :]
    launch(0)

    def relayout(y, carry):
        for c in range(3):
            for x in range(X):
                for t in range(K // 8):
                    row = (c * X + x) * Y + y + t * 8 * rows
                    panel[c, x, y, t * 8 : t * 8 + 8, :] = z_ref[pl.ds(row, 8, stride=rows), :]
        return carry

    lax.fori_loop(0, Y, relayout, 0)

    def far_refs(d):
        sx, sy = neighbours[d]
        px, py = (0 if sx < 0 else X - 1), (0 if sy < 0 else Y - 1)
        if sx and sy:
            return panel.at[:, px, py], lambda e: far_c.at[(0, 1, 2, 3)[(0, 2, 5, 7).index(e)]]
        if sx:
            return panel.at[:, px], lambda e: far_x.at[0 if e == 1 else 1]
        return panel.at[:, :, py], lambda e: far_y.at[0 if e == 3 else 1]

    def far_copy(d, landing):
        source, slot = far_refs(d)
        return pltpu.make_async_remote_copy(
            src_ref=source,
            dst_ref=slot(landing),
            send_sem=far_send.at[d],
            recv_sem=far_recv.at[landing],
            device_id=peer(d),
            device_id_type=MESH,
        )

    for d in range(8):

        @pl.when(exists(d))
        def _():
            far_copy(d, 7 - d).start()

    def diagonal(t, carry):
        first = pl.multiple_of(t * 8, 8)
        v = [panel[c, :, :, pl.ds(first, 8), :] for c in range(3)]
        scale = (27.0 + s_ref[...])[:, :, None, :]
        total = jnp.zeros_like(v[0])
        for c in range(3):
            across = v[c] + shift_lead(v[c], 1, 0) + shift_lead(v[c], -1, 0)
            across = across + shift_lead(across, 1, 1) + shift_lead(across, -1, 1)
            total = total + v[c] * (scale * v[c] - across) - 2.0 * shift_z(v[c], 1) * across
        dz2 = shift_z(v[2], 1) - shift_z(v[2], -1)
        dy1 = shift_lead(v[1], 1, 1) - shift_lead(v[1], -1, 1)
        both = dy1 + dz2
        dx = shift_lead(both, 1, 0) - shift_lead(both, -1, 0)
        dy = shift_lead(dz2, 1, 1) - shift_lead(dz2, -1, 1)
        total = total + 2.0 * mixing * (v[0] * dx + v[1] * dy)
        part = jnp.sum(total.reshape(X * Y, 8, Z), axis=0)
        whole = jnp.sum(part, axis=1, keepdims=True)
        weight[pl.ds(first, 8), :] = jnp.broadcast_to(damping / whole, (8, Z))
        return carry

    lax.fori_loop(0, K // 8, diagonal, 0)

    def restrict(field):
        def body(y, acc):
            for c in range(3):
                for x in range(X):
                    acc = acc + panel[c, x, y] * field[c, x, pl.ds(y, 1), :]
            return acc

        acc = lax.fori_loop(0, Y, body, jnp.zeros((K, Z), jnp.float32))
        return jnp.broadcast_to(jnp.sum(acc, axis=1, keepdims=True), (K, Z))

    def prolong(vector):
        coarse[...] = vector

        def body(k, acc):
            block = z_ref[pl.ds(pl.multiple_of(k * rows, 8), rows), :].reshape(3 * X, Y, Z)
            return acc + block * coarse[pl.ds(k, 1), :][None]

        acc = lax.fori_loop(0, K, body, jnp.zeros((3 * X, Y, Z), jnp.float32), unroll=4)
        return acc.reshape(3, X, Y, Z)

    def put_own(target, field):
        for c in range(3):
            target[c, 2 : X + 2, 0:Y, :] = field[c]

    def operate(field):
        out = stencil(ext, 2, X)
        scale = 27.0 + s_ref[...]
        return [scale * field[c] + out[c][:, 0:Y] for c in range(3)]

    def precondition(turn, current, result):
        first = weight[...] * restrict(current)
        own_p[...] = prolong(first)
        pack_own(turn + 1, own_p)
        launch(turn + 1)
        await_all(turn)
        put_own(ext_r, current)
        unpack_halo(turn, ext_r)
        if turn == 0:
            wide = X + 2
            ext_inv[1 : X + 3] = jnp.zeros((wide, 16, Z), jnp.float32)
            ext_inv[2 : X + 2, 0:Y, :] = s_ref[...]
            for d, (sx, sy) in enumerate(neighbours):
                px, py = (1 if sx < 0 else X + 2), (15 if sy < 0 else 8)
                if sx and sy:
                    ext_inv[px, py, :] = recv[0, d, 3, :]
                elif sx:
                    ext_inv[px, 0:Y] = recv[0, d, 3 * Y : 4 * Y, :]
                else:
                    for x in range(X):
                        ext_inv[2 + x, py, :] = recv[0, d, 3 * X + x, :]
            row = lax.broadcasted_iota(jnp.int32, (wide, 16, Z), 1)
            inside = jnp.logical_or(row <= 8, row == 15)
            ext_inv[1 : X + 3] = jnp.where(inside, damping / (26.0 + ext_inv[1 : X + 3]), 0.0)
        inv = ext_inv[1 : X + 3]
        for c in range(3):
            ext[c, 1 : X + 3] = inv * ext_r[c, 1 : X + 3]
        for _ in range(SWEEPS - 1):
            out = stencil(ext, 1, X + 2)
            new = [
                (1.0 - damping) * ext[c, 1 : X + 3] + inv * (ext_r[c, 1 : X + 3] - ext[c, 1 : X + 3] - out[c])
                for c in range(3)
            ]
            for c in range(3):
                ext[c, 1 : X + 3] = new[c]
        pack_ring(turn + 2)
        launch(turn + 2)
        for c in range(3):
            result[c] = ext[c, 2 : X + 2, 0:Y]
        await_all(turn + 1)
        put_own(ext, own_p)
        unpack_halo(turn + 1, ext)
        image = operate(own_p)
        for c in range(3):
            own_u[c] = current[c] - image[c]
        result[...] += prolong(first + weight[...] * restrict(own_u))
        await_all(turn + 2)
        add_ring(turn + 2, result)

    def image_of(turn, field, result):
        pack_own(turn, field)
        launch(turn)
        put_own(ext, field)
        await_all(turn)
        unpack_halo(turn, ext)
        out = operate(field)
        for c in range(3):
            result[c] = out[c]

    precondition(0, r_ref, own_z)
    image_of(3, own_z, own_w)
    pack_own(4, own_w)
    launch(4)
    precondition(4, own_w, own_v)
    image_of(7, own_v, own_u)

    pairs = ((r_ref, own_z), (own_z, own_w), (r_ref, own_v), (own_w, own_v), (own_z, own_u), (own_v, own_u))
    for i, (a, b) in enumerate(pairs):
        part = jnp.sum((a[...] * b[...]).reshape(3 * X, Y, Z), axis=0)
        dots[i : i + 1, :] = jnp.sum(part, axis=0, keepdims=True)

    def exchange(axis_pos, me, size, buffer, s_sem, r_sem):
        def target(o):
            other = lax.rem(me + o, size)
            return (other, (other, gy) if axis_pos == 0 else (gx, other))

        def copy(o, slot):
            other, where = target(o)
            return pltpu.make_async_remote_copy(
                src_ref=dots,
                dst_ref=buffer.at[me if slot is None else other],
                send_sem=s_sem.at[o],
                recv_sem=r_sem.at[me if slot is None else other],
                device_id=where,
                device_id_type=MESH,
            )

        for o in range(1, size):
            copy(o, None).start()
        buffer[me] = dots[...]
        for o in range(1, size):
            copy(o, 1).wait_recv()
        for o in range(1, size):
            copy(o, None).wait_send()
        dots[...] = jnp.sum(buffer[...], axis=0)

    exchange(0, gx, n_gx, sums_x, sx_send, sx_recv)
    exchange(1, gy, n_gy, sums_y, sy_send, sy_recv)
    total = jnp.sum(dots[...], axis=1, keepdims=True)
    rz, zw, rv, wv, zu, vu = (total[i : i + 1, :] for i in range(6))
    step0 = rz / zw
    rz_new = step0 * (step0 * wv - rv)
    grow = 1.0 + rz_new / rz
    step1 = rz_new / (grow * grow * zw - grow * step0 * (wv + zu) + step0 * step0 * vu)
    keep = jnp.broadcast_to(step0 + step1 * grow, (Y, Z))[None, None]
    cross = jnp.broadcast_to(step1 * step0, (Y, Z))[None, None]
    x_out[...] = keep * own_z[...] - cross * own_v[...]
    res_out[...] = r_ref[...] - keep * own_w[...] + cross * own_u[...]

    for d, (sx, sy) in enumerate(neighbours):
        cells = 1 if sx and sy else (Y if sx else X)

        @pl.when(exists(d))
        def _():
            source, slot = far_refs(d)
            far_copy(d, d).wait_recv()
            other = slot(d)
            if sx and sy:
                parts = ring_image([source[c].reshape(1, K, Z) for c in range(3)], sx, sy)
            else:
                parts = ring_image([source[c] for c in range(3)], sx, sy)
            for c in range(3):
                image_x[c, 0:cells] = parts[c]

            def body(i, acc):
                for c in range(3):
                    right = other[c] if sx and sy else other[c, i]
                    acc = acc + lax.dot_general(
                        split_rows(image_x[c, i]), split_rows(right), (((1,), (1,)), ((), ())),
                        preferred_element_type=jnp.float32,
                    )
                return acc

            acc = lax.fori_loop(0, cells, body, jnp.zeros((2 * K, 2 * K), jnp.float32))
            half = acc[0:K] + acc[K : 2 * K]
            tile_out[d] = half[:, 0:K] + half[:, K : 2 * K]

        @pl.when(jnp.logical_not(exists(d)))
        def _():
            tile_out[d] = jnp.zeros((K, K), jnp.float32)

    for d in range(8):

        @pl.when(exists(d))
        def _():
            far_copy(d, 7 - d).wait_send()
            for turn in range(ROUNDS):
                message(turn, d).wait_send()


def per_device(n_gx, n_gy, right_side, stiffness, panels):
    X, Y, Z = stiffness.shape
    K = panels.shape[0]
    f32 = jnp.float32
    field = pltpu.VMEM((3, X, Y, Z), f32)
    dma = pltpu.SemaphoreType.DMA
    vmem = pl.BlockSpec(memory_space=pltpu.VMEM)
    x, res, tiles = pl.pallas_call(
        functools.partial(kernel, n_gx, n_gy),
        out_shape=(
            jax.ShapeDtypeStruct((3, X, Y, Z), f32),
            jax.ShapeDtypeStruct((3, X, Y, Z), f32),
            jax.ShapeDtypeStruct((8, K, K), f32),
        ),
        in_specs=[vmem] * 3,
        out_specs=(vmem,) * 3,
        scratch_shapes=[
            pltpu.VMEM((3, X, Y, K, Z), f32),
            pltpu.VMEM((2, 3, Y, K, Z), f32),
            pltpu.VMEM((2, 3, X, K, Z), f32),
            pltpu.VMEM((4, 3, K, Z), f32),
            pltpu.VMEM((3, Y, K, Z), f32),
            pltpu.VMEM((ROUNDS, 8, 32, Z), f32),
            pltpu.VMEM((ROUNDS, 8, 32, Z), f32),
            pltpu.VMEM((3, X + 4, 16, Z), f32),
            pltpu.VMEM((3, X + 4, 16, Z), f32),
            pltpu.VMEM((X + 4, 16, Z), f32),
            field, field, field, field, field,
            pltpu.VMEM((K, Z), f32),
            pltpu.VMEM((K, Z), f32),
            pltpu.VMEM((8, Z), f32),
            pltpu.VMEM((n_gx, 8, Z), f32),
            pltpu.VMEM((n_gy, 8, Z), f32),
            dma((ROUNDS, 8)), dma((ROUNDS, 8)), dma((8,)), dma((8,)),
            dma((n_gx,)), dma((n_gx,)), dma((n_gy,)), dma((n_gy,)),
        ],
        compiler_params=pltpu.CompilerParams(
            collective_id=0, has_side_effects=True, vmem_limit_bytes=48 * 1024 * 1024
        ),
    )(right_side, stiffness, panels.reshape(K * 3 * X * Y, Z))
    return x, res, tiles.reshape(1, 1, 8, K * K)


def solution(mesh):
    n_gx, n_gy = mesh.shape["gx"], mesh.shape["gy"]
    return jax.shard_map(
        functools.partial(per_device, n_gx, n_gy),
        mesh=mesh,
        in_specs=(P(None, "gx", "gy", None), P("gx", "gy", None), P(None, None, "gx", "gy", None)),
        out_specs=(P(None, "gx", "gy", None), P(None, "gx", "gy", None), P("gx", "gy", None, None)),
        check_vma=False,
    )
```

```python
import functools

import jax
import jax.numpy as jnp
from jax import lax
from jax.experimental import pallas as pl
from jax.experimental.pallas import tpu as pltpu
from jax.sharding import PartitionSpec as P

SWEEPS = 4
MESH = pl.DeviceIdType.MESH
mixing = 0.25
damping = 0.5
neighbours = ((-1, -1), (-1, 0), (-1, 1), (0, -1), (0, 1), (1, -1), (1, 0), (1, 1))
ROUNDS = 8


def shift_z(value, step):
    axis = value.ndim - 1
    size = value.shape[axis]
    rolled = pltpu.roll(value, (-step) % size, axis)
    lane = lax.broadcasted_iota(jnp.int32, value.shape, axis)
    edge = size - 1 if step == 1 else 0
    return jnp.where(lane == edge, 0.0, rolled)


def shift_lead(value, step, axis):
    size = value.shape[axis]
    zero = jnp.zeros_like(lax.slice_in_dim(value, 0, 1, axis=axis))
    if step == 1:
        return jnp.concatenate([lax.slice_in_dim(value, 1, size, axis=axis), zero], axis=axis)
    return jnp.concatenate([zero, lax.slice_in_dim(value, 0, size - 1, axis=axis)], axis=axis)


def stencil(field, start, count):
    def planes(c, step):
        return field[c, start + step : start + step + count]

    def up(v):
        return pltpu.roll(v, 15, 1)

    def down(v):
        return pltpu.roll(v, 1, 1)

    low = [planes(c, -1) for c in range(3)]
    mid = [planes(c, 0) for c in range(3)]
    high = [planes(c, 1) for c in range(3)]
    box = []
    for c in range(3):
        along = low[c] + mid[c] + high[c]
        box.append(along + up(along) + down(along))
    dx0, dx1, dx2 = (high[c] - low[c] for c in range(3))
    dy1 = up(mid[1]) - down(mid[1])
    dz2 = shift_z(mid[2], 1) - shift_z(mid[2], -1)
    side0 = mixing * dx2
    out0 = (
        mixing * (up(dx1) - down(dx1)) - box[0] + shift_z(side0 - box[0], 1) - shift_z(side0 + box[0], -1)
    )
    side1 = mixing * (dx0 + dz2)
    out1 = up(side1) - down(side1) - box[1] - shift_z(box[1], 1) - shift_z(box[1], -1)
    side2 = mixing * (dx0 + dy1)
    out2 = shift_z(side2 - box[2], 1) - shift_z(side2 + box[2], -1) - box[2]
    return out0, out1, out2


def ring_image(edge, sx, sy):
    boxes = []
    for c in range(3):
        v = edge[c]
        if sx == 0 or sy == 0:
            v = v + shift_lead(v, 1, 0) + shift_lead(v, -1, 0)
        boxes.append(v + shift_z(v, 1) + shift_z(v, -1))
    if sx and sy:
        return [mixing * sx * sy * edge[1] - boxes[0], mixing * sx * sy * edge[0] - boxes[1], -boxes[2]]

    def along(v):
        return shift_lead(v, 1, 0) - shift_lead(v, -1, 0)

    def third(v):
        return shift_z(v, 1) - shift_z(v, -1)

    if sx:
        return [
            -mixing * sx * (along(edge[1]) + third(edge[2])) - boxes[0],
            -mixing * sx * along(edge[0]) - boxes[1],
            -mixing * sx * third(edge[0]) - boxes[2],
        ]
    return [
        -mixing * sy * along(edge[1]) - boxes[0],
        -mixing * sy * (along(edge[0]) + third(edge[2])) - boxes[1],
        -mixing * sy * third(edge[1]) - boxes[2],
    ]


def split_rows(value):
    high = value.astype(jnp.bfloat16)
    low = (value - high.astype(jnp.float32)).astype(jnp.bfloat16)
    return jnp.concatenate([high, low], axis=0)


def kernel(
    n_gx, n_gy, r_hbm, s_hbm, z_hbm, x_out, res_out, tile_out,
    r_ref, s_ref, z_ref, panel, far_x, far_y, far_c, image_x, image_y, image_c, share, share_far, send, recv, ext, ext_r, ext_inv, own_p, own_z, own_w, own_v, own_u,
    weight, coarse, dots, sums_x, sums_y,
    in_sem, send_sem, recv_sem, far_send, far_recv, part_send, part_recv, sx_send, sx_recv, sy_send, sy_recv,
):
    X, Y, Z = s_ref.shape
    K = panel.shape[3]
    rows = 3 * X * Y
    gx, gy = lax.axis_index("gx"), lax.axis_index("gy")

    def exists(d):
        sx, sy = neighbours[d]
        ok = jnp.bool_(True)
        if sx < 0:
            ok = gx > 0
        if sx > 0:
            ok = gx < n_gx - 1
        if sy:
            ok_y = gy > 0 if sy < 0 else gy < n_gy - 1
            ok = jnp.logical_and(ok, ok_y) if sx else ok_y
        return ok

    def peer(d):
        return (gx + neighbours[d][0], gy + neighbours[d][1])

    load_z = pltpu.make_async_copy(z_hbm, z_ref, in_sem.at[0])
    load_r = pltpu.make_async_copy(r_hbm, r_ref, in_sem.at[1])
    load_s = pltpu.make_async_copy(s_hbm, s_ref, in_sem.at[2])
    load_r.start()
    load_s.start()
    load_z.start()
    recv[...] = jnp.zeros_like(recv)
    ext[...] = jnp.zeros_like(ext)
    ext_r[...] = jnp.zeros_like(ext_r)
    ext_inv[...] = jnp.zeros_like(ext_inv)
    dots[...] = jnp.zeros_like(dots)
    barrier = pltpu.get_barrier_semaphore()
    count = jnp.int32(n_gx - 1 + n_gy - 1)
    for o in range(1, n_gx):
        pl.semaphore_signal(barrier, inc=1, device_id=(lax.rem(gx + o, n_gx), gy), device_id_type=MESH)
    for o in range(1, n_gy):
        pl.semaphore_signal(barrier, inc=1, device_id=(gx, lax.rem(gy + o, n_gy)), device_id_type=MESH)
    for d in (0, 2, 5, 7):
        count = count + exists(d).astype(jnp.int32)

        @pl.when(exists(d))
        def _():
            pl.semaphore_signal(barrier, inc=1, device_id=peer(d), device_id_type=MESH)

    load_r.wait()
    load_s.wait()
    pl.semaphore_wait(barrier, count)

    def length(d, with_stiff):
        sx, sy = neighbours[d]
        if sx and sy:
            return 8
        if sx:
            return 32 if with_stiff else 24
        return 16

    def message(turn, d):
        n = length(d, turn == 0)
        return pltpu.make_async_remote_copy(
            src_ref=send.at[turn, d, 0:n],
            dst_ref=recv.at[turn, 7 - d, 0:n],
            send_sem=send_sem.at[turn, d],
            recv_sem=recv_sem.at[turn, 7 - d],
            device_id=peer(d),
            device_id_type=MESH,
        )

    def arrival(turn, d):
        n = length(d, turn == 0)
        return pltpu.make_async_remote_copy(
            src_ref=send.at[turn, d, 0:n],
            dst_ref=recv.at[turn, d, 0:n],
            send_sem=send_sem.at[turn, d],
            recv_sem=recv_sem.at[turn, d],
            device_id=peer(d),
            device_id_type=MESH,
        )

    def launch(turn):
        for d in range(8):

            @pl.when(exists(d))
            def _():
                message(turn, d).start()

    def await_all(turn):
        for d in range(8):

            @pl.when(exists(d))
            def _():
                arrival(turn, d).wait_recv()

    def pack_own(turn, field):
        for d, (sx, sy) in enumerate(neighbours):
            px, py = (0 if sx < 0 else X - 1), (0 if sy < 0 else Y - 1)
            for c in range(3):
                if sx and sy:
                    send[turn, d, c, :] = field[c, px, py, :]
                elif sx:
                    send[turn, d, c * Y : (c + 1) * Y, :] = field[c, px]
                else:
                    for x in range(X):
                        send[turn, d, c * X + x, :] = field[c, x, py, :]

    def pack_ring(turn):
        for d, (sx, sy) in enumerate(neighbours):
            px, py = (1 if sx < 0 else X + 2), (15 if sy < 0 else 8)
            for c in range(3):
                if sx and sy:
                    send[turn, d, c, :] = ext[c, px, py, :]
                elif sx:
                    send[turn, d, c * Y : (c + 1) * Y, :] = ext[c, px, 0:Y]
                else:
                    for x in range(X):
                        send[turn, d, c * X + x, :] = ext[c, 2 + x, py, :]

    def unpack_halo(turn, target):
        for d, (sx, sy) in enumerate(neighbours):
            px, py = (1 if sx < 0 else X + 2), (15 if sy < 0 else 8)
            for c in range(3):
                if sx and sy:
                    target[c, px, py, :] = recv[turn, d, c, :]
                elif sx:
                    target[c, px, 0:Y] = recv[turn, d, c * Y : (c + 1) * Y, :]
                else:
                    for x in range(X):
                        target[c, 2 + x, py, :] = recv[turn, d, c * X + x, :]

    def add_ring(turn, target):
        for d, (sx, sy) in enumerate(neighbours):
            px, py = (0 if sx < 0 else X - 1), (0 if sy < 0 else Y - 1)
            for c in range(3):
                if sx and sy:
                    target[c, px, py, :] += recv[turn, d, c, :]
                elif sx:
                    target[c, px] += recv[turn, d, c * Y : (c + 1) * Y, :]
                else:
                    for x in range(X):
                        target[c, x, py, :] += recv[turn, d, c * X + x, :]

    pack_own(0, r_ref)
    for d, (sx, sy) in enumerate(neighbours):
        px, py = (0 if sx < 0 else X - 1), (0 if sy < 0 else Y - 1)
        if sx and sy:
            send[0, d, 3, :] = s_ref[px, py, :]
        elif sx:
            send[0, d, 3 * Y : 4 * Y, :] = s_ref[px]
        else:
            for x in range(X):
                send[0, d, 3 * X + x, :] = s_ref[x, py, :]
    launch(0)

    def relayout(y, carry):
        for c in range(3):
            for x in range(X):
                for t in range(K // 8):
                    row = (c * X + x) * Y + y + t * 8 * rows
                    panel[c, x, y, t * 8 : t * 8 + 8, :] = z_ref[pl.ds(row, 8, stride=rows), :]
        return carry

    load_z.wait()
    lax.fori_loop(0, Y, relayout, 0)

    hx, hy = X // 2, Y // 2

    def far_copy(d):
        source, slot = {
            1: lambda: (panel.at[:, 0, 0:hy], far_x.at[1]),
            3: lambda: (panel.at[:, 0:hx, 0], far_y.at[1]),
            0: lambda: (panel.at[:, 0, 0], far_c.at[1]),
            6: lambda: (image_x.at[:, hy:Y], far_x.at[0]),
            4: lambda: (image_y.at[:, hx:X], far_y.at[0]),
            5: lambda: (image_c.at[0], far_c.at[0]),
        }[d]()
        return pltpu.make_async_remote_copy(
            src_ref=source, dst_ref=slot, send_sem=far_send.at[d], recv_sem=far_recv.at[7 - d],
            device_id=peer(d), device_id_type=MESH,
        )

    def far_arrival(d):
        slot = {6: (far_x, 1), 4: (far_y, 1), 7: (far_c, 1), 1: (far_x, 0), 3: (far_y, 0), 2: (far_c, 0)}[d]
        here = slot[0].at[slot[1]]
        return pltpu.make_async_remote_copy(
            src_ref=here, dst_ref=here, send_sem=far_send.at[d], recv_sem=far_recv.at[d],
            device_id=peer(d), device_id_type=MESH,
        )

    def far_start(d):
        @pl.when(exists(d))
        def _():
            far_copy(d).start()

    def make_image(d):
        sx, sy = neighbours[d]
        px, py = (0 if sx < 0 else X - 1), (0 if sy < 0 else Y - 1)

        @pl.when(exists(d))
        def _():
            if sx and sy:
                parts = ring_image([panel[c, px, py].reshape(1, K, Z) for c in range(3)], sx, sy)
                for c in range(3):
                    image_c[0 if d == 5 else 1, c] = parts[c].reshape(K, Z)
            elif sx:
                parts = ring_image([panel[c, px] for c in range(3)], sx, sy)
                for c in range(3):
                    image_x[c] = parts[c]
            else:
                parts = ring_image([panel[c, :, py] for c in range(3)], sx, sy)
                for c in range(3):
                    image_y[c] = parts[c]

    def part_copy(d):
        return pltpu.make_async_remote_copy(
            src_ref=share.at[d], dst_ref=share_far.at[7 - d], send_sem=part_send.at[d], recv_sem=part_recv.at[7 - d],
            device_id=peer(d), device_id_type=MESH,
        )

    def part_arrival(d):
        return pltpu.make_async_remote_copy(
            src_ref=share.at[d], dst_ref=share_far.at[d], send_sem=part_send.at[d], recv_sem=part_recv.at[d],
            device_id=peer(d), device_id_type=MESH,
        )

    def make_part(d):
        @pl.when(exists(d))
        def _():
            far_arrival(d).wait_recv()
            left, right = [], []
            for c in range(3):
                if d == 6:
                    for y in range(hy):
                        left.append(image_x[c, y])
                        right.append(far_x[1, c, y])
                elif d == 4:
                    for x in range(hx):
                        left.append(image_y[c, x])
                        right.append(far_y[1, c, x])
                elif d == 7:
                    left.append(image_c[1, c])
                    right.append(far_c[1, c])
                elif d == 1:
                    for y in range(hy, Y):
                        left.append(far_x[0, c, y - hy])
                        right.append(panel[c, 0, y])
                elif d == 3:
                    for x in range(hx, X):
                        left.append(far_y[0, c, x - hx])
                        right.append(panel[c, x, 0])
                else:
                    left.append(far_c[0, c])
                    right.append(panel[c, 0, Y - 1])
            acc = lax.dot_general(
                jnp.concatenate([split_rows(v) for v in left], axis=1),
                jnp.concatenate([split_rows(v) for v in right], axis=1),
                (((1,), (1,)), ((), ())),
                preferred_element_type=jnp.float32,
            )
            half = acc[0:K] + acc[K : 2 * K]
            tile = half[:, 0:K] + half[:, K : 2 * K]
            share[d] = jnp.concatenate([tile[0 : K // 2], tile[K // 2 : K]], axis=1)
            part_copy(d).start()

    for d in (1, 3, 0):
        far_start(d)

    def diagonal(t, carry):
        first = pl.multiple_of(t * 8, 8)
        v = [panel[c, :, :, pl.ds(first, 8), :] for c in range(3)]
        scale = (27.0 + s_ref[...])[:, :, None, :]
        total = jnp.zeros_like(v[0])
        for c in range(3):
            across = v[c] + shift_lead(v[c], 1, 0) + shift_lead(v[c], -1, 0)
            across = across + shift_lead(across, 1, 1) + shift_lead(across, -1, 1)
            total = total + v[c] * (scale * v[c] - across) - 2.0 * shift_z(v[c], 1) * across
        dz2 = shift_z(v[2], 1) - shift_z(v[2], -1)
        dy1 = shift_lead(v[1], 1, 1) - shift_lead(v[1], -1, 1)
        both = dy1 + dz2
        dx = shift_lead(both, 1, 0) - shift_lead(both, -1, 0)
        dy = shift_lead(dz2, 1, 1) - shift_lead(dz2, -1, 1)
        total = total + 2.0 * mixing * (v[0] * dx + v[1] * dy)
        part = jnp.sum(total.reshape(X * Y, 8, Z), axis=0)
        whole = jnp.sum(part, axis=1, keepdims=True)
        weight[pl.ds(first, 8), :] = jnp.broadcast_to(damping / whole, (8, Z))
        return carry

    lax.fori_loop(0, K // 8, diagonal, 0)

    def restrict(field):
        def body(y, acc):
            for c in range(3):
                for x in range(X):
                    acc = acc + panel[c, x, y] * field[c, x, pl.ds(y, 1), :]
            return acc

        acc = lax.fori_loop(0, Y, body, jnp.zeros((K, Z), jnp.float32))
        return jnp.broadcast_to(jnp.sum(acc, axis=1, keepdims=True), (K, Z))

    def prolong(vector):
        coarse[...] = vector

        def body(k, acc):
            block = z_ref[pl.ds(pl.multiple_of(k * rows, 8), rows), :].reshape(3 * X, Y, Z)
            return acc + block * coarse[pl.ds(k, 1), :][None]

        acc = lax.fori_loop(0, K, body, jnp.zeros((3 * X, Y, Z), jnp.float32), unroll=4)
        return acc.reshape(3, X, Y, Z)

    def put_own(target, field):
        for c in range(3):
            target[c, 2 : X + 2, 0:Y, :] = field[c]

    def operate(field):
        out = stencil(ext, 2, X)
        scale = 27.0 + s_ref[...]
        return [scale * field[c] + out[c][:, 0:Y] for c in range(3)]

    def precondition(turn, current, result):
        first = weight[...] * restrict(current)
        own_p[...] = prolong(first)
        pack_own(turn + 1, own_p)
        launch(turn + 1)
        await_all(turn)
        put_own(ext_r, current)
        unpack_halo(turn, ext_r)
        if turn == 0:
            wide = X + 2
            ext_inv[1 : X + 3] = jnp.zeros((wide, 16, Z), jnp.float32)
            ext_inv[2 : X + 2, 0:Y, :] = s_ref[...]
            for d, (sx, sy) in enumerate(neighbours):
                px, py = (1 if sx < 0 else X + 2), (15 if sy < 0 else 8)
                if sx and sy:
                    ext_inv[px, py, :] = recv[0, d, 3, :]
                elif sx:
                    ext_inv[px, 0:Y] = recv[0, d, 3 * Y : 4 * Y, :]
                else:
                    for x in range(X):
                        ext_inv[2 + x, py, :] = recv[0, d, 3 * X + x, :]
            row = lax.broadcasted_iota(jnp.int32, (wide, 16, Z), 1)
            inside = jnp.logical_or(row <= 8, row == 15)
            ext_inv[1 : X + 3] = jnp.where(inside, damping / (26.0 + ext_inv[1 : X + 3]), 0.0)
        inv = ext_inv[1 : X + 3]
        for c in range(3):
            ext[c, 1 : X + 3] = inv * ext_r[c, 1 : X + 3]
        for _ in range(SWEEPS - 1):
            out = stencil(ext, 1, X + 2)
            new = [
                (1.0 - damping) * ext[c, 1 : X + 3] + inv * (ext_r[c, 1 : X + 3] - ext[c, 1 : X + 3] - out[c])
                for c in range(3)
            ]
            for c in range(3):
                ext[c, 1 : X + 3] = new[c]
        pack_ring(turn + 2)
        launch(turn + 2)
        if turn == 0:
            make_image(6)
            far_start(6)
        else:
            for d in (1, 2, 3):
                make_part(d)
        for c in range(3):
            result[c] = ext[c, 2 : X + 2, 0:Y]
        await_all(turn + 1)
        put_own(ext, own_p)
        unpack_halo(turn + 1, ext)
        image = operate(own_p)
        for c in range(3):
            own_u[c] = current[c] - image[c]
        result[...] += prolong(first + weight[...] * restrict(own_u))
        await_all(turn + 2)
        add_ring(turn + 2, result)

    def image_of(turn, field, result):
        pack_own(turn, field)
        launch(turn)
        put_own(ext, field)
        if turn == 3:
            make_image(4)
            far_start(4)
            make_image(5)
            far_start(5)
            make_image(7)
        await_all(turn)
        unpack_halo(turn, ext)
        out = operate(field)
        for c in range(3):
            result[c] = out[c]

    precondition(0, r_ref, own_z)
    image_of(3, own_z, own_w)
    pack_own(4, own_w)
    launch(4)
    for d in (6, 4, 7):
        make_part(d)
    precondition(4, own_w, own_v)
    image_of(7, own_v, own_u)

    pairs = ((r_ref, own_z), (own_z, own_w), (r_ref, own_v), (own_w, own_v), (own_z, own_u), (own_v, own_u))
    for i, (a, b) in enumerate(pairs):
        part = jnp.sum((a[...] * b[...]).reshape(3 * X, Y, Z), axis=0)
        dots[i : i + 1, :] = jnp.sum(part, axis=0, keepdims=True)

    def exchange(axis_pos, me, size, buffer, s_sem, r_sem):
        def target(o):
            other = lax.rem(me + o, size)
            return (other, (other, gy) if axis_pos == 0 else (gx, other))

        def copy(o, slot):
            other, where = target(o)
            return pltpu.make_async_remote_copy(
                src_ref=dots,
                dst_ref=buffer.at[me if slot is None else other],
                send_sem=s_sem.at[o],
                recv_sem=r_sem.at[me if slot is None else other],
                device_id=where,
                device_id_type=MESH,
            )

        for o in range(1, size):
            copy(o, None).start()
        buffer[me] = dots[...]
        for o in range(1, size):
            copy(o, 1).wait_recv()
        for o in range(1, size):
            copy(o, None).wait_send()
        dots[...] = jnp.sum(buffer[...], axis=0)

    exchange(0, gx, n_gx, sums_x, sx_send, sx_recv)
    exchange(1, gy, n_gy, sums_y, sy_send, sy_recv)
    total = jnp.sum(dots[...], axis=1, keepdims=True)
    rz, zw, rv, wv, zu, vu = (total[i : i + 1, :] for i in range(6))
    step0 = rz / zw
    rz_new = step0 * (step0 * wv - rv)
    grow = 1.0 + rz_new / rz
    step1 = rz_new / (grow * grow * zw - grow * step0 * (wv + zu) + step0 * step0 * vu)
    keep = jnp.broadcast_to(step0 + step1 * grow, (Y, Z))[None, None]
    cross = jnp.broadcast_to(step1 * step0, (Y, Z))[None, None]
    x_out[...] = keep * own_z[...] - cross * own_v[...]
    res_out[...] = r_ref[...] - keep * own_w[...] + cross * own_u[...]

    for d in range(8):

        @pl.when(exists(d))
        def _():
            whole = share[d] if d in (2, 7) else None
            if d not in (2, 7):
                part_arrival(d).wait_recv()
                whole = share_far[d] if d in (0, 5) else share[d] + share_far[d]
            tile = jnp.concatenate([whole[:, 0:K], whole[:, K : 2 * K]], axis=0)
            tile_out[d] = tile if d >= 4 else tile.T

        @pl.when(jnp.logical_not(exists(d)))
        def _():
            tile_out[d] = jnp.zeros((K, K), jnp.float32)

    for d in range(8):

        @pl.when(exists(d))
        def _():
            if d not in (2, 7):
                far_copy(d).wait_send()
            if d not in (0, 5):
                part_copy(d).wait_send()
            for turn in range(ROUNDS):
                message(turn, d).wait_send()


def per_device(n_gx, n_gy, right_side, stiffness, panels):
    X, Y, Z = stiffness.shape
    K = panels.shape[0]
    f32 = jnp.float32
    field = pltpu.VMEM((3, X, Y, Z), f32)
    dma = pltpu.SemaphoreType.DMA
    vmem = pl.BlockSpec(memory_space=pltpu.VMEM)
    x, res, tiles = pl.pallas_call(
        functools.partial(kernel, n_gx, n_gy),
        out_shape=(
            jax.ShapeDtypeStruct((3, X, Y, Z), f32),
            jax.ShapeDtypeStruct((3, X, Y, Z), f32),
            jax.ShapeDtypeStruct((8, K, K), f32),
        ),
        in_specs=[pl.BlockSpec(memory_space=pl.ANY)] * 3,
        out_specs=(vmem,) * 3,
        scratch_shapes=[
            field,
            pltpu.VMEM((X, Y, Z), f32),
            pltpu.VMEM((K * 3 * X * Y, Z), f32),
            pltpu.VMEM((3, X, Y, K, Z), f32),
            pltpu.VMEM((2, 3, Y // 2, K, Z), f32),
            pltpu.VMEM((2, 3, X // 2, K, Z), f32),
            pltpu.VMEM((2, 3, K, Z), f32),
            pltpu.VMEM((3, Y, K, Z), f32),
            pltpu.VMEM((3, X, K, Z), f32),
            pltpu.VMEM((2, 3, K, Z), f32),
            pltpu.VMEM((8, K // 2, 2 * K), f32),
            pltpu.VMEM((8, K // 2, 2 * K), f32),
            pltpu.VMEM((ROUNDS, 8, 32, Z), f32),
            pltpu.VMEM((ROUNDS, 8, 32, Z), f32),
            pltpu.VMEM((3, X + 4, 16, Z), f32),
            pltpu.VMEM((3, X + 4, 16, Z), f32),
            pltpu.VMEM((X + 4, 16, Z), f32),
            field, field, field, field, field,
            pltpu.VMEM((K, Z), f32),
            pltpu.VMEM((K, Z), f32),
            pltpu.VMEM((8, Z), f32),
            pltpu.VMEM((n_gx, 8, Z), f32),
            pltpu.VMEM((n_gy, 8, Z), f32),
            dma((3,)), dma((ROUNDS, 8)), dma((ROUNDS, 8)), dma((8,)), dma((8,)), dma((8,)), dma((8,)),
            dma((n_gx,)), dma((n_gx,)), dma((n_gy,)), dma((n_gy,)),
        ],
        compiler_params=pltpu.CompilerParams(
            collective_id=0, has_side_effects=True, vmem_limit_bytes=56 * 1024 * 1024
        ),
    )(right_side, stiffness, panels.reshape(K * 3 * X * Y, Z))
    return x, res, tiles.reshape(1, 1, 8, K * K)


def solution(mesh):
    n_gx, n_gy = mesh.shape["gx"], mesh.shape["gy"]
    return jax.shard_map(
        functools.partial(per_device, n_gx, n_gy),
        mesh=mesh,
        in_specs=(P(None, "gx", "gy", None), P("gx", "gy", None), P(None, None, "gx", "gy", None)),
        out_specs=(P(None, "gx", "gy", None), P(None, "gx", "gy", None), P("gx", "gy", None, None)),
        check_vma=False,
    )
```

```python
import functools

import jax
import jax.numpy as jnp
from jax import lax
from jax.experimental import pallas as pl
from jax.experimental.pallas import tpu as pltpu
from jax.sharding import PartitionSpec as P

SWEEPS = 4
MESH = pl.DeviceIdType.MESH
mixing = 0.25
damping = 0.5
neighbours = ((-1, -1), (-1, 0), (-1, 1), (0, -1), (0, 1), (1, -1), (1, 0), (1, 1))
ROUNDS = 6
STRIPS = (2, 5)


def shift_z(value, step):
    axis = value.ndim - 1
    size = value.shape[axis]
    rolled = pltpu.roll(value, (-step) % size, axis)
    lane = lax.broadcasted_iota(jnp.int32, value.shape, axis)
    edge = size - 1 if step == 1 else 0
    return jnp.where(lane == edge, 0.0, rolled)


def shift_lead(value, step, axis):
    size = value.shape[axis]
    zero = jnp.zeros_like(lax.slice_in_dim(value, 0, 1, axis=axis))
    if step == 1:
        return jnp.concatenate([lax.slice_in_dim(value, 1, size, axis=axis), zero], axis=axis)
    return jnp.concatenate([zero, lax.slice_in_dim(value, 0, size - 1, axis=axis)], axis=axis)


def stencil(field, wide, start, count):
    def planes(c, step):
        first = (c * wide + start + step) * 16
        return field[first : first + count * 16, :].reshape(count, 16, field.shape[1])

    def up(v):
        return pltpu.roll(v, 15, 1)

    def down(v):
        return pltpu.roll(v, 1, 1)

    low = [planes(c, -1) for c in range(3)]
    mid = [planes(c, 0) for c in range(3)]
    high = [planes(c, 1) for c in range(3)]
    box = []
    for c in range(3):
        along = low[c] + mid[c] + high[c]
        box.append(along + up(along) + down(along))
    dx0, dx1, dx2 = (high[c] - low[c] for c in range(3))
    dy1 = up(mid[1]) - down(mid[1])
    dz2 = shift_z(mid[2], 1) - shift_z(mid[2], -1)
    side0 = mixing * dx2
    out0 = (
        mixing * (up(dx1) - down(dx1)) - box[0] + shift_z(side0 - box[0], 1) - shift_z(side0 + box[0], -1)
    )
    side1 = mixing * (dx0 + dz2)
    out1 = up(side1) - down(side1) - box[1] - shift_z(box[1], 1) - shift_z(box[1], -1)
    side2 = mixing * (dx0 + dy1)
    out2 = shift_z(side2 - box[2], 1) - shift_z(side2 + box[2], -1) - box[2]
    return out0, out1, out2


def ring_image(edge, sx, sy):
    boxes = []
    for c in range(3):
        v = edge[c]
        if sx == 0 or sy == 0:
            v = v + shift_lead(v, 1, 0) + shift_lead(v, -1, 0)
        boxes.append(v + shift_z(v, 1) + shift_z(v, -1))
    if sx and sy:
        return [mixing * sx * sy * edge[1] - boxes[0], mixing * sx * sy * edge[0] - boxes[1], -boxes[2]]

    def along(v):
        return shift_lead(v, 1, 0) - shift_lead(v, -1, 0)

    def third(v):
        return shift_z(v, 1) - shift_z(v, -1)

    if sx:
        return [
            -mixing * sx * (along(edge[1]) + third(edge[2])) - boxes[0],
            -mixing * sx * along(edge[0]) - boxes[1],
            -mixing * sx * third(edge[0]) - boxes[2],
        ]
    return [
        -mixing * sy * along(edge[1]) - boxes[0],
        -mixing * sy * (along(edge[0]) + third(edge[2])) - boxes[1],
        -mixing * sy * third(edge[1]) - boxes[2],
    ]


def split_rows(value):
    high = value.astype(jnp.bfloat16)
    low = (value - high.astype(jnp.float32)).astype(jnp.bfloat16)
    return jnp.concatenate([high, low], axis=0)


def kernel(
    n_gx, n_gy, r_hbm, s_hbm, z_hbm, x_out, res_out, tile_out,
    r_ref, s_ref, z_ref, panel, far_x, far_y, far_c, image_x, image_y, image_c, share, share_far, send, recv, ext, ext_r, ext_p, ext_inv, own_p, own_z, own_w, own_v, own_u,
    weight, coarse, square, packed, dots, sums_x, sums_y,
    in_sem, send_sem, recv_sem, far_send, far_recv, part_send, part_recv, sx_send, sx_recv, sy_send, sy_recv,
):
    X, Y, K, Z = panel.shape[1:]
    wide = X + 4
    rows = 3 * X * Y
    gx, gy = lax.axis_index("gx"), lax.axis_index("gy")

    def exists(d):
        sx, sy = neighbours[d]
        ok = jnp.bool_(True)
        if sx < 0:
            ok = gx > 0
        if sx > 0:
            ok = gx < n_gx - 1
        if sy:
            ok_y = gy > 0 if sy < 0 else gy < n_gy - 1
            ok = jnp.logical_and(ok, ok_y) if sx else ok_y
        return ok

    def peer(d):
        return (gx + neighbours[d][0], gy + neighbours[d][1])

    load_z = pltpu.make_async_copy(z_hbm, z_ref, in_sem.at[0])
    load_r = pltpu.make_async_copy(r_hbm, r_ref, in_sem.at[1])
    load_s = pltpu.make_async_copy(s_hbm, s_ref, in_sem.at[2])
    load_r.start()
    load_s.start()
    load_z.start()
    recv[...] = jnp.zeros_like(recv)
    ext[...] = jnp.zeros_like(ext)
    ext_r[...] = jnp.zeros_like(ext_r)
    ext_p[...] = jnp.zeros_like(ext_p)
    ext_inv[...] = jnp.zeros_like(ext_inv)
    dots[...] = jnp.zeros_like(dots)
    barrier = pltpu.get_barrier_semaphore()
    count = jnp.int32(n_gx - 1 + n_gy - 1)
    for o in range(1, n_gx):
        pl.semaphore_signal(barrier, inc=1, device_id=(lax.rem(gx + o, n_gx), gy), device_id_type=MESH)
    for o in range(1, n_gy):
        pl.semaphore_signal(barrier, inc=1, device_id=(gx, lax.rem(gy + o, n_gy)), device_id_type=MESH)
    for d in (0, 2, 5, 7):
        count = count + exists(d).astype(jnp.int32)

        @pl.when(exists(d))
        def _():
            pl.semaphore_signal(barrier, inc=1, device_id=peer(d), device_id_type=MESH)

    load_r.wait()
    load_s.wait()

    def relayout(y, carry):
        for c in range(3):
            for x in range(X):
                for t in range(K // 8):
                    row = (c * X + x) * Y + y + t * 8 * rows
                    panel[c, x, y, t * 8 : t * 8 + 8, :] = z_ref[pl.ds(row, 8, stride=rows), :]
        return carry

    load_z.wait()
    lax.fori_loop(0, Y, relayout, 0)

    pl.semaphore_wait(barrier, count)

    def length(turn, d):
        sx, sy = neighbours[d]
        if turn in STRIPS:
            return 16 if sx and sy else (64 if sx else 48)
        if sx and sy:
            return 8
        if sx:
            return 32 if turn == 0 else 24
        return 16

    def message(turn, d):
        n = length(turn, d)
        return pltpu.make_async_remote_copy(
            src_ref=send.at[turn, d, 0:n],
            dst_ref=recv.at[turn, 7 - d, 0:n],
            send_sem=send_sem.at[turn, d],
            recv_sem=recv_sem.at[turn, 7 - d],
            device_id=peer(d),
            device_id_type=MESH,
        )

    def arrival(turn, d):
        n = length(turn, d)
        return pltpu.make_async_remote_copy(
            src_ref=send.at[turn, d, 0:n],
            dst_ref=recv.at[turn, d, 0:n],
            send_sem=send_sem.at[turn, d],
            recv_sem=recv_sem.at[turn, d],
            device_id=peer(d),
            device_id_type=MESH,
        )

    def launch(turn):
        for d in range(8):

            @pl.when(exists(d))
            def _():
                message(turn, d).start()

    def await_all(turn):
        for d in range(8):

            @pl.when(exists(d))
            def _():
                arrival(turn, d).wait_recv()

    def pack_own(turn, field):
        for d, (sx, sy) in enumerate(neighbours):
            px, py = (0 if sx < 0 else X - 1), (0 if sy < 0 else Y - 1)
            if sx and sy:
                send[turn, d, 0:3, :] = field[pl.ds(px * Y + py, 3, stride=X * Y), :]
                continue
            for c in range(3):
                if sx:
                    first = (c * X + px) * Y
                    send[turn, d, c * Y : (c + 1) * Y, :] = field[first : first + Y, :]
                else:
                    send[turn, d, c * X : (c + 1) * X, :] = field[pl.ds(c * X * Y + py, X, stride=Y), :]

    def unpack_halo(turn, target):
        for d, (sx, sy) in enumerate(neighbours):
            px, py = (1 if sx < 0 else X + 2), (15 if sy < 0 else 8)
            if sx and sy:
                target[pl.ds(px * 16 + py, 3, stride=wide * 16), :] = recv[turn, d, 0:3, :]
                continue
            for c in range(3):
                if sx:
                    first = (c * wide + px) * 16
                    target[first : first + Y, :] = recv[turn, d, c * Y : (c + 1) * Y, :]
                else:
                    first = (c * wide + 2) * 16 + py
                    target[pl.ds(first, X, stride=16), :] = recv[turn, d, c * X : (c + 1) * X, :]

    def strips(turn, visit):
        for d, (sx, sy) in enumerate(neighbours):
            p0, ys = (1 if sx < 0 else X + 1), ((15, 0) if sy < 0 else (7, 8))
            if sx == 0:
                for c in range(3):
                    for t in range(2):
                        first = (c * 2 + t) * 8
                        visit(d, pl.ds((c * wide + 1) * 16 + ys[t], X + 2, stride=16), slice(first, first + X + 2))
                continue
            if sy == 0:
                for c in range(3):
                    for p in range(2):
                        first, row = (c * 2 + p) * 8, (c * wide + p0 + p) * 16
                        visit(d, slice(row, row + 8), slice(first, first + 8))
                ys = (15, 8)
            base = 48 if sy == 0 else 0
            for p in range(2):
                for t in range(2):
                    first = base + (p * 2 + t) * 4
                    visit(d, pl.ds((p0 + p) * 16 + ys[t], 3, stride=wide * 16), slice(first, first + 3))

    def pack_strips(turn):
        def visit(d, here, there):
            send[turn, d, there, :] = ext[here, :]

        strips(turn, visit)

    def add_strips(turn):
        def visit(d, here, there):
            ext[here, :] = ext[here, :] + recv[turn, d, there, :]

        strips(turn, visit)
        for ok, plane in ((gx == 0, 1), (gx == n_gx - 1, X + 2)):

            @pl.when(ok)
            def _():
                for c in range(3):
                    first = (c * wide + plane) * 16
                    ext[first : first + 16, :] = jnp.zeros((16, Z), jnp.float32)

        for ok, row in ((gy == 0, 15), (gy == n_gy - 1, 8)):

            @pl.when(ok)
            def _():
                for c in range(3):
                    first = (c * wide + 1) * 16 + row
                    ext[pl.ds(first, X + 2, stride=16), :] = jnp.zeros((X + 2, Z), jnp.float32)

    pack_own(0, r_ref)
    for d, (sx, sy) in enumerate(neighbours):
        px, py = (0 if sx < 0 else X - 1), (0 if sy < 0 else Y - 1)
        if sx and sy:
            send[0, d, 3:4, :] = s_ref[px * Y + py : px * Y + py + 1, :]
        elif sx:
            send[0, d, 3 * Y : 4 * Y, :] = s_ref[px * Y : (px + 1) * Y, :]
        else:
            send[0, d, 3 * X : 4 * X, :] = s_ref[pl.ds(py, X, stride=Y), :]
    launch(0)

    hx, hy = X // 2, Y // 2

    def far_copy(d):
        source, slot = {
            1: lambda: (panel.at[:, 0, 0:hy], far_x.at[1]),
            3: lambda: (panel.at[:, 0:hx, 0], far_y.at[1]),
            0: lambda: (panel.at[:, 0, 0], far_c.at[1]),
            6: lambda: (image_x.at[:, hy:Y], far_x.at[0]),
            4: lambda: (image_y.at[:, hx:X], far_y.at[0]),
            5: lambda: (image_c.at[0], far_c.at[0]),
        }[d]()
        return pltpu.make_async_remote_copy(
            src_ref=source, dst_ref=slot, send_sem=far_send.at[d], recv_sem=far_recv.at[7 - d],
            device_id=peer(d), device_id_type=MESH,
        )

    def far_arrival(d):
        slot = {6: (far_x, 1), 4: (far_y, 1), 7: (far_c, 1), 1: (far_x, 0), 3: (far_y, 0), 2: (far_c, 0)}[d]
        here = slot[0].at[slot[1]]
        return pltpu.make_async_remote_copy(
            src_ref=here, dst_ref=here, send_sem=far_send.at[d], recv_sem=far_recv.at[d],
            device_id=peer(d), device_id_type=MESH,
        )

    def far_start(d):
        @pl.when(exists(d))
        def _():
            far_copy(d).start()

    def make_image(d):
        sx, sy = neighbours[d]
        px, py = (0 if sx < 0 else X - 1), (0 if sy < 0 else Y - 1)

        @pl.when(exists(d))
        def _():
            if sx and sy:
                parts = ring_image([panel[c, px, py].reshape(1, K, Z) for c in range(3)], sx, sy)
                for c in range(3):
                    image_c[0 if d == 5 else 1, c] = parts[c].reshape(K, Z)
            elif sx:
                parts = ring_image([panel[c, px] for c in range(3)], sx, sy)
                for c in range(3):
                    image_x[c] = parts[c]
            else:
                parts = ring_image([panel[c, :, py] for c in range(3)], sx, sy)
                for c in range(3):
                    image_y[c] = parts[c]

    def part_copy(d):
        return pltpu.make_async_remote_copy(
            src_ref=share.at[d], dst_ref=share_far.at[7 - d], send_sem=part_send.at[d], recv_sem=part_recv.at[7 - d],
            device_id=peer(d), device_id_type=MESH,
        )

    def part_arrival(d):
        return pltpu.make_async_remote_copy(
            src_ref=share.at[d], dst_ref=share_far.at[d], send_sem=part_send.at[d], recv_sem=part_recv.at[d],
            device_id=peer(d), device_id_type=MESH,
        )

    def make_part(d):
        @pl.when(exists(d))
        def _():
            far_arrival(d).wait_recv()
            left, right = [], []
            for c in range(3):
                if d == 6:
                    for y in range(hy):
                        left.append(image_x[c, y])
                        right.append(far_x[1, c, y])
                elif d == 4:
                    for x in range(hx):
                        left.append(image_y[c, x])
                        right.append(far_y[1, c, x])
                elif d == 7:
                    left.append(image_c[1, c])
                    right.append(far_c[1, c])
                elif d == 1:
                    for y in range(hy, Y):
                        left.append(far_x[0, c, y - hy])
                        right.append(panel[c, 0, y])
                elif d == 3:
                    for x in range(hx, X):
                        left.append(far_y[0, c, x - hx])
                        right.append(panel[c, x, 0])
                else:
                    left.append(far_c[0, c])
                    right.append(panel[c, 0, Y - 1])
            acc = lax.dot_general(
                jnp.concatenate([split_rows(v) for v in left], axis=1),
                jnp.concatenate([split_rows(v) for v in right], axis=1),
                (((1,), (1,)), ((), ())),
                preferred_element_type=jnp.float32,
            )
            half = acc[0:K] + acc[K : 2 * K]
            tile = half[:, 0:K] + half[:, K : 2 * K]
            share[d] = jnp.concatenate([tile[0 : K // 2], tile[K // 2 : K]], axis=1)
            part_copy(d).start()

    for d in (1, 3, 0):
        far_start(d)

    def diagonal(t, carry):
        first = pl.multiple_of(t * 8, 8)
        v = [panel[c, :, :, pl.ds(first, 8), :] for c in range(3)]
        scale = (27.0 + s_ref[...].reshape(X, Y, Z))[:, :, None, :]
        total = jnp.zeros_like(v[0])
        for c in range(3):
            across = v[c] + shift_lead(v[c], 1, 0) + shift_lead(v[c], -1, 0)
            across = across + shift_lead(across, 1, 1) + shift_lead(across, -1, 1)
            total = total + v[c] * (scale * v[c] - across) - 2.0 * shift_z(v[c], 1) * across
        dz2 = shift_z(v[2], 1) - shift_z(v[2], -1)
        dy1 = shift_lead(v[1], 1, 1) - shift_lead(v[1], -1, 1)
        both = dy1 + dz2
        dx = shift_lead(both, 1, 0) - shift_lead(both, -1, 0)
        dy = shift_lead(dz2, 1, 1) - shift_lead(dz2, -1, 1)
        total = total + 2.0 * mixing * (v[0] * dx + v[1] * dy)
        part = jnp.sum(total.reshape(X * Y, 8, Z), axis=0)
        whole = jnp.sum(part, axis=1, keepdims=True)
        weight[pl.ds(first, 8), :] = jnp.broadcast_to(damping / whole, (8, Z))
        return carry

    lax.fori_loop(0, K // 8, diagonal, 0)

    def restrict(field):
        def body(y, acc):
            for c in range(3):
                for x in range(X):
                    acc = acc + panel[c, x, y] * field[pl.ds((c * X + x) * Y + y, 1), :]
            return acc

        acc = lax.fori_loop(0, Y, body, jnp.zeros((K, Z), jnp.float32))
        return jnp.broadcast_to(jnp.sum(acc, axis=1, keepdims=True), (K, Z))

    def prolong(vector):
        coarse[...] = vector

        def body(k, acc):
            block = z_ref[pl.ds(pl.multiple_of(k * rows, 8), rows), :].reshape(3 * X, Y, Z)
            return acc + block * coarse[pl.ds(k, 1), :][None]

        acc = lax.fori_loop(0, K, body, jnp.zeros((3 * X, Y, Z), jnp.float32), unroll=4)
        return acc.reshape(rows, Z)

    def put_own(target, field):
        for c in range(3):
            for x in range(X):
                here, there = (c * wide + 2 + x) * 16, (c * X + x) * Y
                target[here : here + Y, :] = field[there : there + Y, :]

    def operate(padded, field):
        out = stencil(padded, wide, 2, X)
        scale = 27.0 + s_ref[...]
        per = X * Y
        return [scale * field[c * per : (c + 1) * per, :] + out[c][:, 0:Y].reshape(per, Z) for c in range(3)]

    def inner(ref, c):
        first = (c * wide + 1) * 16
        return slice(first, first + (X + 2) * 16)

    def apply_both(turn, current, result, image, filler):
        first = weight[...] * restrict(current)
        own_p[...] = prolong(first)
        pack_own(turn + 1, own_p)
        launch(turn + 1)
        put_own(ext_r, current)
        put_own(ext_p, own_p)
        await_all(turn)
        unpack_halo(turn, ext_r)
        if turn == 0:
            for x in range(X):
                ext_inv[(2 + x) * 16 : (2 + x) * 16 + Y, :] = s_ref[x * Y : (x + 1) * Y, :]
            for d, (sx, sy) in enumerate(neighbours):
                px, py = (1 if sx < 0 else X + 2), (15 if sy < 0 else 8)
                if sx and sy:
                    ext_inv[px * 16 + py : px * 16 + py + 1, :] = recv[0, d, 3:4, :]
                elif sx:
                    ext_inv[px * 16 : px * 16 + Y, :] = recv[0, d, 3 * Y : 4 * Y, :]
                else:
                    ext_inv[pl.ds(2 * 16 + py, X, stride=16), :] = recv[0, d, 3 * X : 4 * X, :]
            shape = ((X + 2) * 16, Z)
            row = lax.rem(lax.broadcasted_iota(jnp.int32, shape, 0), 16)
            inside = jnp.logical_or(row <= 8, row == 15)
            stiff = ext_inv[16 : (X + 3) * 16, :]
            ext_inv[16 : (X + 3) * 16, :] = jnp.where(inside, damping / (26.0 + stiff), 0.0)
        inv = ext_inv[16 : (X + 3) * 16, :]
        for c in range(3):
            ext[inner(ext, c), :] = inv * ext_r[inner(ext, c), :]
        for _ in range(SWEEPS - 1):
            out = stencil(ext, wide, 1, X + 2)
            new = []
            for c in range(3):
                e = ext[inner(ext, c), :]
                change = ext_r[inner(ext, c), :] - e - out[c].reshape((X + 2) * 16, Z)
                new.append((1.0 - damping) * e + inv * change)
            for c in range(3):
                ext[inner(ext, c), :] = new[c]
        await_all(turn + 1)
        unpack_halo(turn + 1, ext_p)
        coarse_image = operate(ext_p, own_p)
        per = X * Y
        for c in range(3):
            own_u[c * per : (c + 1) * per, :] = current[c * per : (c + 1) * per, :] - coarse_image[c]
        own_p[...] = prolong(first + weight[...] * restrict(own_u))
        for c in range(3):
            for x in range(X):
                here, there = (c * wide + 2 + x) * 16, (c * X + x) * Y
                ext[here : here + Y, :] = ext[here : here + Y, :] + own_p[there : there + Y, :]
        pack_strips(turn + 2)
        launch(turn + 2)
        filler()
        await_all(turn + 2)
        add_strips(turn + 2)
        for c in range(3):
            for x in range(X):
                here, there = (c * wide + 2 + x) * 16, (c * X + x) * Y
                result[there : there + Y, :] = ext[here : here + Y, :]
        out = operate(ext, result)
        for c in range(3):
            image[c * per : (c + 1) * per, :] = out[c]

    def fill_images():
        for d in (6, 4, 5):
            make_image(d)
            far_start(d)
        make_image(7)

    def fill_parts():
        for d in (6, 4, 7):
            make_part(d)

    apply_both(0, r_ref, own_z, own_w, fill_images)
    pack_own(3, own_w)
    launch(3)
    apply_both(3, own_w, own_v, own_u, fill_parts)

    pairs = ((r_ref, own_z), (own_z, own_w), (r_ref, own_v), (own_w, own_v), (own_z, own_u), (own_v, own_u))
    for i, (a, b) in enumerate(pairs):
        part = jnp.sum((a[...] * b[...]).reshape(3 * X, 8, Z), axis=0)
        dots[i : i + 1, :] = jnp.sum(part, axis=0, keepdims=True)

    def exchange(axis_pos, me, size, buffer, s_sem, r_sem, filler):
        def target(o):
            other = lax.rem(me + o, size)
            return (other, (other, gy) if axis_pos == 0 else (gx, other))

        def copy(o, slot):
            other, where = target(o)
            return pltpu.make_async_remote_copy(
                src_ref=dots,
                dst_ref=buffer.at[me if slot is None else other],
                send_sem=s_sem.at[o],
                recv_sem=r_sem.at[me if slot is None else other],
                device_id=where,
                device_id_type=MESH,
            )

        for o in range(1, size):
            copy(o, None).start()
        buffer[me] = dots[...]
        filler()
        for o in range(1, size):
            copy(o, 1).wait_recv()
        for o in range(1, size):
            copy(o, None).wait_send()
        dots[...] = jnp.sum(buffer[...], axis=0)

    def later_parts():
        for d in (1, 3, 2):
            make_part(d)

    def finish(d):
        @pl.when(exists(d))
        def _():
            whole = share[d] if d in (2, 7) else None
            if d not in (2, 7):
                part_arrival(d).wait_recv()
                whole = share_far[d] if d in (0, 5) else share[d] + share_far[d]
            tile = jnp.concatenate([whole[:, 0:K], whole[:, K : 2 * K]], axis=0)
            square[:, 0:K] = tile if d >= 4 else tile.T
            even = square[pl.ds(0, K // 2, stride=2), :]
            odd = square[pl.ds(1, K // 2, stride=2), :]
            packed[d * K // 2 : (d + 1) * K // 2, :] = jnp.concatenate([even[:, 0:K], odd[:, 0:K]], axis=1)

        @pl.when(jnp.logical_not(exists(d)))
        def _():
            packed[d * K // 2 : (d + 1) * K // 2, :] = jnp.zeros((K // 2, 2 * K), jnp.float32)

    def early_tiles():
        for d in (7, 2):
            finish(d)

    exchange(0, gx, n_gx, sums_x, sx_send, sx_recv, later_parts)
    exchange(1, gy, n_gy, sums_y, sy_send, sy_recv, early_tiles)
    total = jnp.sum(dots[...], axis=1, keepdims=True)
    rz, zw, rv, wv, zu, vu = (total[i : i + 1, :] for i in range(6))
    step0 = rz / zw
    rz_new = step0 * (step0 * wv - rv)
    grow = 1.0 + rz_new / rz
    step1 = rz_new / (grow * grow * zw - grow * step0 * (wv + zu) + step0 * step0 * vu)
    keep = step0 + step1 * grow
    cross = step1 * step0
    x_out[...] = keep * own_z[...] - cross * own_v[...]
    res_out[...] = r_ref[...] - keep * own_w[...] + cross * own_u[...]
    for d in (0, 5, 4, 6, 3, 1):
        finish(d)
    for j in range(K // 2):
        tile_out[:, j * 2 * K : (j + 1) * 2 * K] = packed[pl.ds(j, 8, stride=K // 2), :]

    for d in range(8):

        @pl.when(exists(d))
        def _():
            if d not in (2, 7):
                far_copy(d).wait_send()
            if d not in (0, 5):
                part_copy(d).wait_send()
            for turn in range(ROUNDS):
                message(turn, d).wait_send()


def emit(*refs):
    sems = refs[6]
    copies = [pltpu.make_async_copy(refs[i], refs[3 + i], sems.at[i]) for i in range(3)]
    for copy in copies:
        copy.start()
    for copy in copies:
        copy.wait()


def per_device(n_gx, n_gy, right_side, stiffness, panels):
    X, Y, Z = stiffness.shape
    K = panels.shape[0]
    f32 = jnp.float32
    cells = 3 * X * Y
    field = pltpu.VMEM((cells, Z), f32)
    padded = pltpu.VMEM((3 * (X + 4) * 16, Z), f32)
    dma = pltpu.SemaphoreType.DMA
    vmem = pl.BlockSpec(memory_space=pltpu.VMEM)
    anywhere = pl.BlockSpec(memory_space=pltpu.HBM)
    results = (
        jax.ShapeDtypeStruct((cells, Z), f32),
        jax.ShapeDtypeStruct((cells, Z), f32),
        jax.ShapeDtypeStruct((8, K * K), f32),
    )
    values = pl.pallas_call(
        functools.partial(kernel, n_gx, n_gy),
        out_shape=results,
        in_specs=[anywhere] * 3,
        out_specs=(vmem,) * 3,
        scratch_shapes=[
            field,
            pltpu.VMEM((X * Y, Z), f32),
            pltpu.VMEM((K * cells, Z), f32),
            pltpu.VMEM((3, X, Y, K, Z), f32),
            pltpu.VMEM((2, 3, Y // 2, K, Z), f32),
            pltpu.VMEM((2, 3, X // 2, K, Z), f32),
            pltpu.VMEM((2, 3, K, Z), f32),
            pltpu.VMEM((3, Y, K, Z), f32),
            pltpu.VMEM((3, X, K, Z), f32),
            pltpu.VMEM((2, 3, K, Z), f32),
            pltpu.VMEM((8, K // 2, 2 * K), f32),
            pltpu.VMEM((8, K // 2, 2 * K), f32),
            pltpu.VMEM((ROUNDS, 8, 64, Z), f32),
            pltpu.VMEM((ROUNDS, 8, 64, Z), f32),
            padded, padded, padded,
            pltpu.VMEM(((X + 4) * 16, Z), f32),
            field, field, field, field, field,
            pltpu.VMEM((K, Z), f32),
            pltpu.VMEM((K, Z), f32),
            pltpu.VMEM((K, 2 * K), f32),
            pltpu.VMEM((8 * K // 2, 2 * K), f32),
            pltpu.VMEM((8, Z), f32),
            pltpu.VMEM((n_gx, 8, Z), f32),
            pltpu.VMEM((n_gy, 8, Z), f32),
            dma((3,)), dma((ROUNDS, 8)), dma((ROUNDS, 8)), dma((8,)), dma((8,)), dma((8,)), dma((8,)),
            dma((n_gx,)), dma((n_gx,)), dma((n_gy,)), dma((n_gy,)),
        ],
        compiler_params=pltpu.CompilerParams(
            collective_id=0, has_side_effects=True, vmem_limit_bytes=56 * 1024 * 1024
        ),
    )(right_side.reshape(cells, Z), stiffness.reshape(X * Y, Z), panels.reshape(K * cells, Z))
    x, res, tiles = pl.pallas_call(
        emit,
        out_shape=results,
        in_specs=[anywhere] * 3,
        out_specs=(anywhere,) * 3,
        scratch_shapes=[dma((3,))],
        compiler_params=pltpu.CompilerParams(vmem_limit_bytes=63 * 1024 * 1024),
    )(*values)
    return x.reshape(3, X, Y, Z), res.reshape(3, X, Y, Z), tiles.reshape(1, 1, 8, K * K)


def solution(mesh):
    n_gx, n_gy = mesh.shape["gx"], mesh.shape["gy"]
    return jax.shard_map(
        functools.partial(per_device, n_gx, n_gy),
        mesh=mesh,
        in_specs=(P(None, "gx", "gy", None), P("gx", "gy", None), P(None, None, "gx", "gy", None)),
        out_specs=(P(None, "gx", "gy", None), P(None, "gx", "gy", None), P("gx", "gy", None, None)),
        check_vma=False,
    )
```

```python
import functools

import jax
import jax.numpy as jnp
from jax import lax
from jax.experimental import pallas as pl
from jax.experimental.pallas import tpu as pltpu
from jax.sharding import PartitionSpec as P

SWEEPS = 4
MESH = pl.DeviceIdType.MESH
mixing = 0.25
damping = 0.5
neighbours = ((-1, -1), (-1, 0), (-1, 1), (0, -1), (0, 1), (1, -1), (1, 0), (1, 1))
ROUNDS = 6
STRIPS = (2, 5)


def shift_z(value, step):
    axis = value.ndim - 1
    size = value.shape[axis]
    rolled = pltpu.roll(value, (-step) % size, axis)
    lane = lax.broadcasted_iota(jnp.int32, value.shape, axis)
    edge = size - 1 if step == 1 else 0
    return jnp.where(lane == edge, 0.0, rolled)


def shift_lead(value, step, axis):
    size = value.shape[axis]
    zero = jnp.zeros_like(lax.slice_in_dim(value, 0, 1, axis=axis))
    if step == 1:
        return jnp.concatenate([lax.slice_in_dim(value, 1, size, axis=axis), zero], axis=axis)
    return jnp.concatenate([zero, lax.slice_in_dim(value, 0, size - 1, axis=axis)], axis=axis)


def stencil(field, wide, start, count):
    def planes(c, step):
        first = (c * wide + start + step) * 16
        return field[first : first + count * 16, :].reshape(count, 16, field.shape[1])

    def up(v):
        return pltpu.roll(v, 15, 1)

    def down(v):
        return pltpu.roll(v, 1, 1)

    low = [planes(c, -1) for c in range(3)]
    mid = [planes(c, 0) for c in range(3)]
    high = [planes(c, 1) for c in range(3)]
    box = []
    for c in range(3):
        along = low[c] + mid[c] + high[c]
        box.append(along + up(along) + down(along))
    dx0, dx1, dx2 = (high[c] - low[c] for c in range(3))
    dy1 = up(mid[1]) - down(mid[1])
    dz2 = shift_z(mid[2], 1) - shift_z(mid[2], -1)
    side0 = mixing * dx2
    out0 = (
        mixing * (up(dx1) - down(dx1)) - box[0] + shift_z(side0 - box[0], 1) - shift_z(side0 + box[0], -1)
    )
    side1 = mixing * (dx0 + dz2)
    out1 = up(side1) - down(side1) - box[1] - shift_z(box[1], 1) - shift_z(box[1], -1)
    side2 = mixing * (dx0 + dy1)
    out2 = shift_z(side2 - box[2], 1) - shift_z(side2 + box[2], -1) - box[2]
    return out0, out1, out2


def ring_image(edge, sx, sy):
    boxes = []
    for c in range(3):
        v = edge[c]
        if sx == 0 or sy == 0:
            v = v + shift_lead(v, 1, 0) + shift_lead(v, -1, 0)
        boxes.append(v + shift_z(v, 1) + shift_z(v, -1))
    if sx and sy:
        return [mixing * sx * sy * edge[1] - boxes[0], mixing * sx * sy * edge[0] - boxes[1], -boxes[2]]

    def along(v):
        return shift_lead(v, 1, 0) - shift_lead(v, -1, 0)

    def third(v):
        return shift_z(v, 1) - shift_z(v, -1)

    if sx:
        return [
            -mixing * sx * (along(edge[1]) + third(edge[2])) - boxes[0],
            -mixing * sx * along(edge[0]) - boxes[1],
            -mixing * sx * third(edge[0]) - boxes[2],
        ]
    return [
        -mixing * sy * along(edge[1]) - boxes[0],
        -mixing * sy * (along(edge[0]) + third(edge[2])) - boxes[1],
        -mixing * sy * third(edge[1]) - boxes[2],
    ]


def split_rows(value):
    high = value.astype(jnp.bfloat16)
    low = (value - high.astype(jnp.float32)).astype(jnp.bfloat16)
    return jnp.concatenate([high, low], axis=0)


def kernel(
    n_gx, n_gy, r_hbm, s_hbm, z_hbm, x_out, res_out, tile_out,
    r_ref, s_ref, z_ref, panel, far_x, far_y, far_c, image_x, image_y, image_c, share, share_far, send, recv, ext, ext_r, ext_p, ext_inv, own_p, own_z, own_w, own_v, own_u,
    weight, coarse, square, packed, dots, sums_x, sums_y,
    in_sem, send_sem, recv_sem, far_send, far_recv, part_send, part_recv, sx_send, sx_recv, sy_send, sy_recv,
):
    X, Y, K, Z = panel.shape[1:]
    wide = X + 4
    rows = 3 * X * Y
    gx, gy = lax.axis_index("gx"), lax.axis_index("gy")

    def exists(d):
        sx, sy = neighbours[d]
        ok = jnp.bool_(True)
        if sx < 0:
            ok = gx > 0
        if sx > 0:
            ok = gx < n_gx - 1
        if sy:
            ok_y = gy > 0 if sy < 0 else gy < n_gy - 1
            ok = jnp.logical_and(ok, ok_y) if sx else ok_y
        return ok

    def peer(d):
        return (gx + neighbours[d][0], gy + neighbours[d][1])

    load_z = pltpu.make_async_copy(z_hbm, z_ref, in_sem.at[0])
    load_r = pltpu.make_async_copy(r_hbm, r_ref, in_sem.at[1])
    load_s = pltpu.make_async_copy(s_hbm, s_ref, in_sem.at[2])
    load_r.start()
    load_s.start()
    load_z.start()
    recv[...] = jnp.zeros_like(recv)
    ext[...] = jnp.zeros_like(ext)
    ext_r[...] = jnp.zeros_like(ext_r)
    ext_p[...] = jnp.zeros_like(ext_p)
    ext_inv[...] = jnp.zeros_like(ext_inv)
    dots[...] = jnp.zeros_like(dots)
    barrier = pltpu.get_barrier_semaphore()
    count = jnp.int32(n_gx - 1 + n_gy - 1)
    for o in range(1, n_gx):
        pl.semaphore_signal(barrier, inc=1, device_id=(lax.rem(gx + o, n_gx), gy), device_id_type=MESH)
    for o in range(1, n_gy):
        pl.semaphore_signal(barrier, inc=1, device_id=(gx, lax.rem(gy + o, n_gy)), device_id_type=MESH)
    for d in (0, 2, 5, 7):
        count = count + exists(d).astype(jnp.int32)

        @pl.when(exists(d))
        def _():
            pl.semaphore_signal(barrier, inc=1, device_id=peer(d), device_id_type=MESH)

    load_r.wait()
    load_s.wait()

    def relayout(y, carry):
        for c in range(3):
            for x in range(X):
                for t in range(K // 8):
                    row = (c * X + x) * Y + y + t * 8 * rows
                    panel[c, x, y, t * 8 : t * 8 + 8, :] = z_ref[pl.ds(row, 8, stride=rows), :]
        return carry

    load_z.wait()
    lax.fori_loop(0, Y, relayout, 0)

    pl.semaphore_wait(barrier, count)

    def length(turn, d):
        sx, sy = neighbours[d]
        if turn in STRIPS:
            return 16 if sx and sy else (64 if sx else 48)
        if sx and sy:
            return 8
        if sx:
            return 32 if turn == 0 else 24
        return 16

    def message(turn, d):
        n = length(turn, d)
        return pltpu.make_async_remote_copy(
            src_ref=send.at[turn, d, 0:n],
            dst_ref=recv.at[turn, 7 - d, 0:n],
            send_sem=send_sem.at[turn, d],
            recv_sem=recv_sem.at[turn, 7 - d],
            device_id=peer(d),
            device_id_type=MESH,
        )

    def arrival(turn, d):
        n = length(turn, d)
        return pltpu.make_async_remote_copy(
            src_ref=send.at[turn, d, 0:n],
            dst_ref=recv.at[turn, d, 0:n],
            send_sem=send_sem.at[turn, d],
            recv_sem=recv_sem.at[turn, d],
            device_id=peer(d),
            device_id_type=MESH,
        )

    def launch(turn):
        for d in range(8):

            @pl.when(exists(d))
            def _():
                message(turn, d).start()

    def await_all(turn):
        for d in range(8):

            @pl.when(exists(d))
            def _():
                arrival(turn, d).wait_recv()

    def pack_own(turn, field):
        for d, (sx, sy) in enumerate(neighbours):
            px, py = (0 if sx < 0 else X - 1), (0 if sy < 0 else Y - 1)
            if sx and sy:
                send[turn, d, 0:3, :] = field[pl.ds(px * Y + py, 3, stride=X * Y), :]
                continue
            for c in range(3):
                if sx:
                    first = (c * X + px) * Y
                    send[turn, d, c * Y : (c + 1) * Y, :] = field[first : first + Y, :]
                else:
                    send[turn, d, c * X : (c + 1) * X, :] = field[pl.ds(c * X * Y + py, X, stride=Y), :]

    def unpack_halo(turn, target):
        for d, (sx, sy) in enumerate(neighbours):
            px, py = (1 if sx < 0 else X + 2), (15 if sy < 0 else 8)
            if sx and sy:
                target[pl.ds(px * 16 + py, 3, stride=wide * 16), :] = recv[turn, d, 0:3, :]
                continue
            for c in range(3):
                if sx:
                    first = (c * wide + px) * 16
                    target[first : first + Y, :] = recv[turn, d, c * Y : (c + 1) * Y, :]
                else:
                    first = (c * wide + 2) * 16 + py
                    target[pl.ds(first, X, stride=16), :] = recv[turn, d, c * X : (c + 1) * X, :]

    def strips(turn, visit):
        for d, (sx, sy) in enumerate(neighbours):
            p0, ys = (1 if sx < 0 else X + 1), ((15, 0) if sy < 0 else (7, 8))
            if sx == 0:
                for c in range(3):
                    for t in range(2):
                        first = (c * 2 + t) * 8
                        visit(d, pl.ds((c * wide + 1) * 16 + ys[t], X + 2, stride=16), slice(first, first + X + 2))
                continue
            if sy == 0:
                for c in range(3):
                    for p in range(2):
                        first, row = (c * 2 + p) * 8, (c * wide + p0 + p) * 16
                        visit(d, slice(row, row + 8), slice(first, first + 8))
                ys = (15, 8)
            base = 48 if sy == 0 else 0
            for p in range(2):
                for t in range(2):
                    first = base + (p * 2 + t) * 4
                    visit(d, pl.ds((p0 + p) * 16 + ys[t], 3, stride=wide * 16), slice(first, first + 3))

    def pack_strips(turn):
        def visit(d, here, there):
            send[turn, d, there, :] = ext[here, :]

        strips(turn, visit)

    def add_strips(turn):
        def visit(d, here, there):
            ext[here, :] = ext[here, :] + recv[turn, d, there, :]

        strips(turn, visit)
        for ok, plane in ((gx == 0, 1), (gx == n_gx - 1, X + 2)):

            @pl.when(ok)
            def _():
                for c in range(3):
                    first = (c * wide + plane) * 16
                    ext[first : first + 16, :] = jnp.zeros((16, Z), jnp.float32)

        for ok, row in ((gy == 0, 15), (gy == n_gy - 1, 8)):

            @pl.when(ok)
            def _():
                for c in range(3):
                    first = (c * wide + 1) * 16 + row
                    ext[pl.ds(first, X + 2, stride=16), :] = jnp.zeros((X + 2, Z), jnp.float32)

    pack_own(0, r_ref)
    for d, (sx, sy) in enumerate(neighbours):
        px, py = (0 if sx < 0 else X - 1), (0 if sy < 0 else Y - 1)
        if sx and sy:
            send[0, d, 3:4, :] = s_ref[px * Y + py : px * Y + py + 1, :]
        elif sx:
            send[0, d, 3 * Y : 4 * Y, :] = s_ref[px * Y : (px + 1) * Y, :]
        else:
            send[0, d, 3 * X : 4 * X, :] = s_ref[pl.ds(py, X, stride=Y), :]
    launch(0)

    hx, hy = X // 2, Y // 2

    def far_copy(d):
        source, slot = {
            1: lambda: (panel.at[:, 0, 0:hy], far_x.at[1]),
            3: lambda: (panel.at[:, 0:hx, 0], far_y.at[1]),
            0: lambda: (panel.at[:, 0, 0], far_c.at[1]),
            6: lambda: (image_x.at[:, hy:Y], far_x.at[0]),
            4: lambda: (image_y.at[:, hx:X], far_y.at[0]),
            5: lambda: (image_c.at[0], far_c.at[0]),
        }[d]()
        return pltpu.make_async_remote_copy(
            src_ref=source, dst_ref=slot, send_sem=far_send.at[d], recv_sem=far_recv.at[7 - d],
            device_id=peer(d), device_id_type=MESH,
        )

    def far_arrival(d):
        slot = {6: (far_x, 1), 4: (far_y, 1), 7: (far_c, 1), 1: (far_x, 0), 3: (far_y, 0), 2: (far_c, 0)}[d]
        here = slot[0].at[slot[1]]
        return pltpu.make_async_remote_copy(
            src_ref=here, dst_ref=here, send_sem=far_send.at[d], recv_sem=far_recv.at[d],
            device_id=peer(d), device_id_type=MESH,
        )

    def far_start(d):
        @pl.when(exists(d))
        def _():
            far_copy(d).start()

    def make_image(d):
        sx, sy = neighbours[d]
        px, py = (0 if sx < 0 else X - 1), (0 if sy < 0 else Y - 1)

        @pl.when(exists(d))
        def _():
            if sx and sy:
                parts = ring_image([panel[c, px, py].reshape(1, K, Z) for c in range(3)], sx, sy)
                for c in range(3):
                    image_c[0 if d == 5 else 1, c] = parts[c].reshape(K, Z)
            else:

                def body(t, carry):
                    group = pl.ds(pl.multiple_of(t * 8, 8), 8)
                    if sx:
                        edge = [panel[c, px, :, group, :] for c in range(3)]
                    else:
                        edge = [panel[c, :, py, group, :] for c in range(3)]
                    parts = ring_image(edge, sx, sy)
                    for c in range(3):
                        if sx:
                            image_x[c, :, group, :] = parts[c]
                        else:
                            image_y[c, :, group, :] = parts[c]
                    return carry

                lax.fori_loop(0, K // 8, body, 0)

    def part_copy(d):
        return pltpu.make_async_remote_copy(
            src_ref=share.at[d], dst_ref=share_far.at[7 - d], send_sem=part_send.at[d], recv_sem=part_recv.at[7 - d],
            device_id=peer(d), device_id_type=MESH,
        )

    def part_arrival(d):
        return pltpu.make_async_remote_copy(
            src_ref=share.at[d], dst_ref=share_far.at[d], send_sem=part_send.at[d], recv_sem=part_recv.at[d],
            device_id=peer(d), device_id_type=MESH,
        )

    def make_part(d):
        @pl.when(exists(d))
        def _():
            far_arrival(d).wait_recv()
            left, right = [], []
            for c in range(3):
                if d == 6:
                    for y in range(hy):
                        left.append(image_x[c, y])
                        right.append(far_x[1, c, y])
                elif d == 4:
                    for x in range(hx):
                        left.append(image_y[c, x])
                        right.append(far_y[1, c, x])
                elif d == 7:
                    left.append(image_c[1, c])
                    right.append(far_c[1, c])
                elif d == 1:
                    for y in range(hy, Y):
                        left.append(far_x[0, c, y - hy])
                        right.append(panel[c, 0, y])
                elif d == 3:
                    for x in range(hx, X):
                        left.append(far_y[0, c, x - hx])
                        right.append(panel[c, x, 0])
                else:
                    left.append(far_c[0, c])
                    right.append(panel[c, 0, Y - 1])
            acc = lax.dot_general(
                jnp.concatenate([split_rows(v) for v in left], axis=1),
                jnp.concatenate([split_rows(v) for v in right], axis=1),
                (((1,), (1,)), ((), ())),
                preferred_element_type=jnp.float32,
            )
            half = acc[0:K] + acc[K : 2 * K]
            tile = half[:, 0:K] + half[:, K : 2 * K]
            share[d] = jnp.concatenate([tile[0 : K // 2], tile[K // 2 : K]], axis=1)
            part_copy(d).start()

    for d in (1, 3, 0):
        far_start(d)
    for d in (6, 4, 5):
        make_image(d)
        far_start(d)
    make_image(7)

    def diagonal(t, carry):
        first = pl.multiple_of(t * 8, 8)

        def at(c, y):
            return panel[c, :, y, pl.ds(first, 8), :]

        total = jnp.zeros((X, 8, Z), jnp.float32)
        for c in range(3):
            sums = [at(c, y) + shift_lead(at(c, y), 1, 0) + shift_lead(at(c, y), -1, 0) for y in range(Y)]
            for y in range(Y):
                v, across = at(c, y), sums[y]
                if y > 0:
                    across = across + sums[y - 1]
                if y < Y - 1:
                    across = across + sums[y + 1]
                scale = jnp.stack(
                    [jnp.broadcast_to(27.0 + s_ref[x * Y + y : x * Y + y + 1, :], (8, Z)) for x in range(X)]
                )
                total = total + v * (scale * v - across) - 2.0 * shift_z(v, 1) * across
        dz2 = [shift_z(at(2, y), 1) - shift_z(at(2, y), -1) for y in range(Y)]
        for y in range(Y):
            both, dy = dz2[y], jnp.zeros((X, 8, Z), jnp.float32)
            if y > 0:
                both, dy = both - at(1, y - 1), dy - dz2[y - 1]
            if y < Y - 1:
                both, dy = both + at(1, y + 1), dy + dz2[y + 1]
            dx = shift_lead(both, 1, 0) - shift_lead(both, -1, 0)
            total = total + 2.0 * mixing * (at(0, y) * dx + at(1, y) * dy)
        part = jnp.sum(total, axis=0)
        whole = jnp.sum(part, axis=1, keepdims=True)
        weight[pl.ds(first, 8), :] = jnp.broadcast_to(damping / whole, (8, Z))
        return carry

    lax.fori_loop(0, K // 8, diagonal, 0)

    def restrict(field):
        def body(y, acc):
            for c in range(3):
                for x in range(X):
                    acc = acc + panel[c, x, y] * field[pl.ds((c * X + x) * Y + y, 1), :]
            return acc

        acc = lax.fori_loop(0, Y, body, jnp.zeros((K, Z), jnp.float32))
        return jnp.broadcast_to(jnp.sum(acc, axis=1, keepdims=True), (K, Z))

    def prolong(vector):
        coarse[...] = vector

        def body(k, acc):
            block = z_ref[pl.ds(pl.multiple_of(k * rows, 8), rows), :].reshape(3 * X, Y, Z)
            return acc + block * coarse[pl.ds(k, 1), :][None]

        acc = lax.fori_loop(0, K, body, jnp.zeros((3 * X, Y, Z), jnp.float32), unroll=4)
        return acc.reshape(rows, Z)

    def put_own(target, field):
        for c in range(3):
            for x in range(X):
                here, there = (c * wide + 2 + x) * 16, (c * X + x) * Y
                target[here : here + Y, :] = field[there : there + Y, :]

    def operate(padded, field):
        out = stencil(padded, wide, 2, X)
        scale = 27.0 + s_ref[...]
        per = X * Y
        return [scale * field[c * per : (c + 1) * per, :] + out[c][:, 0:Y].reshape(per, Z) for c in range(3)]

    def inner(ref, c):
        first = (c * wide + 1) * 16
        return slice(first, first + (X + 2) * 16)

    def apply_both(turn, current, result, image, filler):
        first = weight[...] * restrict(current)
        own_p[...] = prolong(first)
        pack_own(turn + 1, own_p)
        launch(turn + 1)
        put_own(ext_r, current)
        put_own(ext_p, own_p)
        await_all(turn)
        unpack_halo(turn, ext_r)
        if turn == 0:
            for x in range(X):
                ext_inv[(2 + x) * 16 : (2 + x) * 16 + Y, :] = s_ref[x * Y : (x + 1) * Y, :]
            for d, (sx, sy) in enumerate(neighbours):
                px, py = (1 if sx < 0 else X + 2), (15 if sy < 0 else 8)
                if sx and sy:
                    ext_inv[px * 16 + py : px * 16 + py + 1, :] = recv[0, d, 3:4, :]
                elif sx:
                    ext_inv[px * 16 : px * 16 + Y, :] = recv[0, d, 3 * Y : 4 * Y, :]
                else:
                    ext_inv[pl.ds(2 * 16 + py, X, stride=16), :] = recv[0, d, 3 * X : 4 * X, :]
            shape = ((X + 2) * 16, Z)
            row = lax.rem(lax.broadcasted_iota(jnp.int32, shape, 0), 16)
            inside = jnp.logical_or(row <= 8, row == 15)
            stiff = ext_inv[16 : (X + 3) * 16, :]
            ext_inv[16 : (X + 3) * 16, :] = jnp.where(inside, damping / (26.0 + stiff), 0.0)
        inv = ext_inv[16 : (X + 3) * 16, :]
        for c in range(3):
            ext[inner(ext, c), :] = inv * ext_r[inner(ext, c), :]
        for _ in range(SWEEPS - 1):
            out = stencil(ext, wide, 1, X + 2)
            new = []
            for c in range(3):
                e = ext[inner(ext, c), :]
                change = ext_r[inner(ext, c), :] - e - out[c].reshape((X + 2) * 16, Z)
                new.append((1.0 - damping) * e + inv * change)
            for c in range(3):
                ext[inner(ext, c), :] = new[c]
        await_all(turn + 1)
        unpack_halo(turn + 1, ext_p)
        coarse_image = operate(ext_p, own_p)
        per = X * Y
        for c in range(3):
            own_u[c * per : (c + 1) * per, :] = current[c * per : (c + 1) * per, :] - coarse_image[c]
        own_p[...] = prolong(first + weight[...] * restrict(own_u))
        for c in range(3):
            for x in range(X):
                here, there = (c * wide + 2 + x) * 16, (c * X + x) * Y
                ext[here : here + Y, :] = ext[here : here + Y, :] + own_p[there : there + Y, :]
        pack_strips(turn + 2)
        launch(turn + 2)
        filler()
        await_all(turn + 2)
        add_strips(turn + 2)
        for c in range(3):
            for x in range(X):
                here, there = (c * wide + 2 + x) * 16, (c * X + x) * Y
                result[there : there + Y, :] = ext[here : here + Y, :]
        out = operate(ext, result)
        for c in range(3):
            image[c * per : (c + 1) * per, :] = out[c]

    def fill_parts():
        for d in (6, 4, 7):
            make_part(d)

    apply_both(0, r_ref, own_z, own_w, lambda: None)
    pack_own(3, own_w)
    launch(3)
    apply_both(3, own_w, own_v, own_u, fill_parts)

    pairs = ((r_ref, own_z), (own_z, own_w), (r_ref, own_v), (own_w, own_v), (own_z, own_u), (own_v, own_u))
    for i, (a, b) in enumerate(pairs):
        part = jnp.sum((a[...] * b[...]).reshape(3 * X, 8, Z), axis=0)
        dots[i : i + 1, :] = jnp.sum(part, axis=0, keepdims=True)

    def exchange(axis_pos, me, size, buffer, s_sem, r_sem, filler):
        def target(o):
            other = lax.rem(me + o, size)
            return (other, (other, gy) if axis_pos == 0 else (gx, other))

        def copy(o, slot):
            other, where = target(o)
            return pltpu.make_async_remote_copy(
                src_ref=dots,
                dst_ref=buffer.at[me if slot is None else other],
                send_sem=s_sem.at[o],
                recv_sem=r_sem.at[me if slot is None else other],
                device_id=where,
                device_id_type=MESH,
            )

        for o in range(1, size):
            copy(o, None).start()
        buffer[me] = dots[...]
        filler()
        for o in range(1, size):
            copy(o, 1).wait_recv()
        for o in range(1, size):
            copy(o, None).wait_send()
        dots[...] = jnp.sum(buffer[...], axis=0)

    def later_parts():
        for d in (1, 3, 2):
            make_part(d)

    def finish(d):
        @pl.when(exists(d))
        def _():
            whole = share[d] if d in (2, 7) else None
            if d not in (2, 7):
                part_arrival(d).wait_recv()
                whole = share_far[d] if d in (0, 5) else share[d] + share_far[d]
            tile = jnp.concatenate([whole[:, 0:K], whole[:, K : 2 * K]], axis=0)
            square[:, 0:K] = tile if d >= 4 else tile.T
            even = square[pl.ds(0, K // 2, stride=2), :]
            odd = square[pl.ds(1, K // 2, stride=2), :]
            packed[d * K // 2 : (d + 1) * K // 2, :] = jnp.concatenate([even[:, 0:K], odd[:, 0:K]], axis=1)

        @pl.when(jnp.logical_not(exists(d)))
        def _():
            packed[d * K // 2 : (d + 1) * K // 2, :] = jnp.zeros((K // 2, 2 * K), jnp.float32)

    def early_tiles():
        for d in (7, 2):
            finish(d)

    exchange(0, gx, n_gx, sums_x, sx_send, sx_recv, later_parts)
    exchange(1, gy, n_gy, sums_y, sy_send, sy_recv, early_tiles)
    total = jnp.sum(dots[...], axis=1, keepdims=True)
    rz, zw, rv, wv, zu, vu = (total[i : i + 1, :] for i in range(6))
    step0 = rz / zw
    rz_new = step0 * (step0 * wv - rv)
    grow = 1.0 + rz_new / rz
    step1 = rz_new / (grow * grow * zw - grow * step0 * (wv + zu) + step0 * step0 * vu)
    keep = step0 + step1 * grow
    cross = step1 * step0
    x_out[...] = keep * own_z[...] - cross * own_v[...]
    res_out[...] = r_ref[...] - keep * own_w[...] + cross * own_u[...]
    for d in (0, 5, 4, 6, 3, 1):
        finish(d)
    for j in range(K // 2):
        tile_out[:, j * 2 * K : (j + 1) * 2 * K] = packed[pl.ds(j, 8, stride=K // 2), :]

    for d in range(8):

        @pl.when(exists(d))
        def _():
            if d not in (2, 7):
                far_copy(d).wait_send()
            if d not in (0, 5):
                part_copy(d).wait_send()
            for turn in range(ROUNDS):
                message(turn, d).wait_send()


def emit(*refs):
    sems = refs[6]
    copies = [pltpu.make_async_copy(refs[i], refs[3 + i], sems.at[i]) for i in range(3)]
    for copy in copies:
        copy.start()
    for copy in copies:
        copy.wait()


def per_device(n_gx, n_gy, right_side, stiffness, panels):
    X, Y, Z = stiffness.shape
    K = panels.shape[0]
    f32 = jnp.float32
    cells = 3 * X * Y
    field = pltpu.VMEM((cells, Z), f32)
    padded = pltpu.VMEM((3 * (X + 4) * 16, Z), f32)
    dma = pltpu.SemaphoreType.DMA
    vmem = pl.BlockSpec(memory_space=pltpu.VMEM)
    anywhere = pl.BlockSpec(memory_space=pltpu.HBM)
    results = (
        jax.ShapeDtypeStruct((cells, Z), f32),
        jax.ShapeDtypeStruct((cells, Z), f32),
        jax.ShapeDtypeStruct((8, K * K), f32),
    )
    values = pl.pallas_call(
        functools.partial(kernel, n_gx, n_gy),
        out_shape=results,
        in_specs=[anywhere] * 3,
        out_specs=(vmem,) * 3,
        scratch_shapes=[
            field,
            pltpu.VMEM((X * Y, Z), f32),
            pltpu.VMEM((K * cells, Z), f32),
            pltpu.VMEM((3, X, Y, K, Z), f32),
            pltpu.VMEM((2, 3, Y // 2, K, Z), f32),
            pltpu.VMEM((2, 3, X // 2, K, Z), f32),
            pltpu.VMEM((2, 3, K, Z), f32),
            pltpu.VMEM((3, Y, K, Z), f32),
            pltpu.VMEM((3, X, K, Z), f32),
            pltpu.VMEM((2, 3, K, Z), f32),
            pltpu.VMEM((8, K // 2, 2 * K), f32),
            pltpu.VMEM((8, K // 2, 2 * K), f32),
            pltpu.VMEM((ROUNDS, 8, 64, Z), f32),
            pltpu.VMEM((ROUNDS, 8, 64, Z), f32),
            padded, padded, padded,
            pltpu.VMEM(((X + 4) * 16, Z), f32),
            field, field, field, field, field,
            pltpu.VMEM((K, Z), f32),
            pltpu.VMEM((K, Z), f32),
            pltpu.VMEM((K, 2 * K), f32),
            pltpu.VMEM((8 * K // 2, 2 * K), f32),
            pltpu.VMEM((8, Z), f32),
            pltpu.VMEM((n_gx, 8, Z), f32),
            pltpu.VMEM((n_gy, 8, Z), f32),
            dma((3,)), dma((ROUNDS, 8)), dma((ROUNDS, 8)), dma((8,)), dma((8,)), dma((8,)), dma((8,)),
            dma((n_gx,)), dma((n_gx,)), dma((n_gy,)), dma((n_gy,)),
        ],
        compiler_params=pltpu.CompilerParams(
            collective_id=0, has_side_effects=True, vmem_limit_bytes=56 * 1024 * 1024
        ),
    )(right_side.reshape(cells, Z), stiffness.reshape(X * Y, Z), panels.reshape(K * cells, Z))
    x, res, tiles = pl.pallas_call(
        emit,
        out_shape=results,
        in_specs=[anywhere] * 3,
        out_specs=(vmem,) * 3,
        scratch_shapes=[dma((3,))],
        compiler_params=pltpu.CompilerParams(vmem_limit_bytes=63 * 1024 * 1024),
    )(*values)
    return x.reshape(3, X, Y, Z), res.reshape(3, X, Y, Z), tiles.reshape(1, 1, 8, K * K)


def solution(mesh):
    n_gx, n_gy = mesh.shape["gx"], mesh.shape["gy"]
    return jax.shard_map(
        functools.partial(per_device, n_gx, n_gy),
        mesh=mesh,
        in_specs=(P(None, "gx", "gy", None), P("gx", "gy", None), P(None, None, "gx", "gy", None)),
        out_specs=(P(None, "gx", "gy", None), P(None, "gx", "gy", None), P("gx", "gy", None, None)),
        check_vma=False,
    )
```

```python
import functools

import jax
import jax.numpy as jnp
from jax import lax
from jax.experimental import pallas as pl
from jax.experimental.pallas import tpu as pltpu
from jax.sharding import PartitionSpec as P

SWEEPS = 4
MESH = pl.DeviceIdType.MESH
mixing = 0.25
damping = 0.5
neighbours = ((-1, -1), (-1, 0), (-1, 1), (0, -1), (0, 1), (1, -1), (1, 0), (1, 1))
ROUNDS = 6
STRIPS = (2, 5)


def shift_z(value, step):
    axis = value.ndim - 1
    size = value.shape[axis]
    rolled = pltpu.roll(value, (-step) % size, axis)
    lane = lax.broadcasted_iota(jnp.int32, value.shape, axis)
    edge = size - 1 if step == 1 else 0
    return jnp.where(lane == edge, 0.0, rolled)


def shift_lead(value, step, axis):
    size = value.shape[axis]
    zero = jnp.zeros_like(lax.slice_in_dim(value, 0, 1, axis=axis))
    if step == 1:
        return jnp.concatenate([lax.slice_in_dim(value, 1, size, axis=axis), zero], axis=axis)
    return jnp.concatenate([zero, lax.slice_in_dim(value, 0, size - 1, axis=axis)], axis=axis)


def stencil(field, wide, start, count):
    def planes(c, step):
        first = (c * wide + start + step) * 16
        return field[first : first + count * 16, :].reshape(count, 16, field.shape[1])

    def up(v):
        return pltpu.roll(v, 15, 1)

    def down(v):
        return pltpu.roll(v, 1, 1)

    low = [planes(c, -1) for c in range(3)]
    mid = [planes(c, 0) for c in range(3)]
    high = [planes(c, 1) for c in range(3)]
    box = []
    for c in range(3):
        along = low[c] + mid[c] + high[c]
        box.append(along + up(along) + down(along))
    dx0, dx1, dx2 = (high[c] - low[c] for c in range(3))
    dy1 = up(mid[1]) - down(mid[1])
    dz2 = shift_z(mid[2], 1) - shift_z(mid[2], -1)
    side0 = mixing * dx2
    out0 = (
        mixing * (up(dx1) - down(dx1)) - box[0] + shift_z(side0 - box[0], 1) - shift_z(side0 + box[0], -1)
    )
    side1 = mixing * (dx0 + dz2)
    out1 = up(side1) - down(side1) - box[1] - shift_z(box[1], 1) - shift_z(box[1], -1)
    side2 = mixing * (dx0 + dy1)
    out2 = shift_z(side2 - box[2], 1) - shift_z(side2 + box[2], -1) - box[2]
    return out0, out1, out2


def ring_image(edge, sx, sy):
    boxes = []
    for c in range(3):
        v = edge[c]
        if sx == 0 or sy == 0:
            v = v + shift_lead(v, 1, 0) + shift_lead(v, -1, 0)
        boxes.append(v + shift_z(v, 1) + shift_z(v, -1))
    if sx and sy:
        return [mixing * sx * sy * edge[1] - boxes[0], mixing * sx * sy * edge[0] - boxes[1], -boxes[2]]

    def along(v):
        return shift_lead(v, 1, 0) - shift_lead(v, -1, 0)

    def third(v):
        return shift_z(v, 1) - shift_z(v, -1)

    if sx:
        return [
            -mixing * sx * (along(edge[1]) + third(edge[2])) - boxes[0],
            -mixing * sx * along(edge[0]) - boxes[1],
            -mixing * sx * third(edge[0]) - boxes[2],
        ]
    return [
        -mixing * sy * along(edge[1]) - boxes[0],
        -mixing * sy * (along(edge[0]) + third(edge[2])) - boxes[1],
        -mixing * sy * third(edge[1]) - boxes[2],
    ]


def split_rows(value):
    high = value.astype(jnp.bfloat16)
    low = (value - high.astype(jnp.float32)).astype(jnp.bfloat16)
    return jnp.concatenate([high, low], axis=0)


def kernel(
    n_gx, n_gy, r_hbm, s_hbm, z_hbm, x_out, res_out, tile_out,
    r_ref, s_ref, z_ref, panel, far_x, far_y, far_c, image_x, image_y, image_c, share, share_far, send, recv, ext, ext_r, ext_p, ext_inv, own_p, own_z, own_w, own_v, own_u,
    weight, coarse, square, packed, dots, sums_x, sums_y,
    in_sem, send_sem, recv_sem, far_send, far_recv, part_send, part_recv, sx_send, sx_recv, sy_send, sy_recv,
):
    X, Y, K, Z = panel.shape[1:]
    wide = X + 4
    rows = 3 * X * Y
    gx, gy = lax.axis_index("gx"), lax.axis_index("gy")

    def exists(d):
        sx, sy = neighbours[d]
        ok = jnp.bool_(True)
        if sx < 0:
            ok = gx > 0
        if sx > 0:
            ok = gx < n_gx - 1
        if sy:
            ok_y = gy > 0 if sy < 0 else gy < n_gy - 1
            ok = jnp.logical_and(ok, ok_y) if sx else ok_y
        return ok

    def peer(d):
        return (gx + neighbours[d][0], gy + neighbours[d][1])

    load_z = pltpu.make_async_copy(z_hbm, z_ref, in_sem.at[0])
    load_r = pltpu.make_async_copy(r_hbm, r_ref, in_sem.at[1])
    load_s = pltpu.make_async_copy(s_hbm, s_ref, in_sem.at[2])
    load_r.start()
    load_s.start()
    load_z.start()
    recv[...] = jnp.zeros_like(recv)
    ext[...] = jnp.zeros_like(ext)
    ext_r[...] = jnp.zeros_like(ext_r)
    ext_p[...] = jnp.zeros_like(ext_p)
    ext_inv[...] = jnp.zeros_like(ext_inv)
    dots[...] = jnp.zeros_like(dots)
    barrier = pltpu.get_barrier_semaphore()
    count = jnp.int32(n_gx - 1 + n_gy - 1)
    for o in range(1, n_gx):
        pl.semaphore_signal(barrier, inc=1, device_id=(lax.rem(gx + o, n_gx), gy), device_id_type=MESH)
    for o in range(1, n_gy):
        pl.semaphore_signal(barrier, inc=1, device_id=(gx, lax.rem(gy + o, n_gy)), device_id_type=MESH)
    for d in (0, 2, 5, 7):
        count = count + exists(d).astype(jnp.int32)

        @pl.when(exists(d))
        def _():
            pl.semaphore_signal(barrier, inc=1, device_id=peer(d), device_id_type=MESH)

    load_r.wait()
    load_s.wait()

    def relayout(y, carry):
        for c in range(3):
            for x in range(X):
                for t in range(K // 8):
                    row = (c * X + x) * Y + y + t * 8 * rows
                    panel[c, x, y, t * 8 : t * 8 + 8, :] = z_ref[pl.ds(row, 8, stride=rows), :]
        return carry

    load_z.wait()
    lax.fori_loop(0, Y, relayout, 0)

    pl.semaphore_wait(barrier, count)

    def length(turn, d):
        sx, sy = neighbours[d]
        if turn in STRIPS:
            return 16 if sx and sy else (64 if sx else 48)
        if sx and sy:
            return 8
        if sx:
            return 32 if turn == 0 else 24
        return 16

    def message(turn, d):
        n = length(turn, d)
        return pltpu.make_async_remote_copy(
            src_ref=send.at[turn, d, 0:n],
            dst_ref=recv.at[turn, 7 - d, 0:n],
            send_sem=send_sem.at[turn, d],
            recv_sem=recv_sem.at[turn, 7 - d],
            device_id=peer(d),
            device_id_type=MESH,
        )

    def arrival(turn, d):
        n = length(turn, d)
        return pltpu.make_async_remote_copy(
            src_ref=send.at[turn, d, 0:n],
            dst_ref=recv.at[turn, d, 0:n],
            send_sem=send_sem.at[turn, d],
            recv_sem=recv_sem.at[turn, d],
            device_id=peer(d),
            device_id_type=MESH,
        )

    def launch(turn):
        for d in range(8):

            @pl.when(exists(d))
            def _():
                message(turn, d).start()

    def await_all(turn):
        for d in range(8):

            @pl.when(exists(d))
            def _():
                arrival(turn, d).wait_recv()

    def pack_own(turn, field):
        for d, (sx, sy) in enumerate(neighbours):
            px, py = (0 if sx < 0 else X - 1), (0 if sy < 0 else Y - 1)
            if sx and sy:
                send[turn, d, 0:3, :] = field[pl.ds(px * Y + py, 3, stride=X * Y), :]
                continue
            for c in range(3):
                if sx:
                    first = (c * X + px) * Y
                    send[turn, d, c * Y : (c + 1) * Y, :] = field[first : first + Y, :]
                else:
                    send[turn, d, c * X : (c + 1) * X, :] = field[pl.ds(c * X * Y + py, X, stride=Y), :]

    def unpack_halo(turn, target):
        for d, (sx, sy) in enumerate(neighbours):
            px, py = (1 if sx < 0 else X + 2), (15 if sy < 0 else 8)
            if sx and sy:
                target[pl.ds(px * 16 + py, 3, stride=wide * 16), :] = recv[turn, d, 0:3, :]
                continue
            for c in range(3):
                if sx:
                    first = (c * wide + px) * 16
                    target[first : first + Y, :] = recv[turn, d, c * Y : (c + 1) * Y, :]
                else:
                    first = (c * wide + 2) * 16 + py
                    target[pl.ds(first, X, stride=16), :] = recv[turn, d, c * X : (c + 1) * X, :]

    def strips(turn, visit):
        for d, (sx, sy) in enumerate(neighbours):
            p0, ys = (1 if sx < 0 else X + 1), ((15, 0) if sy < 0 else (7, 8))
            if sx == 0:
                for c in range(3):
                    for t in range(2):
                        first = (c * 2 + t) * 8
                        visit(d, pl.ds((c * wide + 1) * 16 + ys[t], X + 2, stride=16), slice(first, first + X + 2))
                continue
            if sy == 0:
                for c in range(3):
                    for p in range(2):
                        first, row = (c * 2 + p) * 8, (c * wide + p0 + p) * 16
                        visit(d, slice(row, row + 8), slice(first, first + 8))
                ys = (15, 8)
            base = 48 if sy == 0 else 0
            for p in range(2):
                for t in range(2):
                    first = base + (p * 2 + t) * 4
                    visit(d, pl.ds((p0 + p) * 16 + ys[t], 3, stride=wide * 16), slice(first, first + 3))

    def pack_strips(turn):
        def visit(d, here, there):
            send[turn, d, there, :] = ext[here, :]

        strips(turn, visit)

    def add_strips(turn):
        def visit(d, here, there):
            ext[here, :] = ext[here, :] + recv[turn, d, there, :]

        strips(turn, visit)
        for ok, plane in ((gx == 0, 1), (gx == n_gx - 1, X + 2)):

            @pl.when(ok)
            def _():
                for c in range(3):
                    first = (c * wide + plane) * 16
                    ext[first : first + 16, :] = jnp.zeros((16, Z), jnp.float32)

        for ok, row in ((gy == 0, 15), (gy == n_gy - 1, 8)):

            @pl.when(ok)
            def _():
                for c in range(3):
                    first = (c * wide + 1) * 16 + row
                    ext[pl.ds(first, X + 2, stride=16), :] = jnp.zeros((X + 2, Z), jnp.float32)

    pack_own(0, r_ref)
    for d, (sx, sy) in enumerate(neighbours):
        px, py = (0 if sx < 0 else X - 1), (0 if sy < 0 else Y - 1)
        if sx and sy:
            send[0, d, 3:4, :] = s_ref[px * Y + py : px * Y + py + 1, :]
        elif sx:
            send[0, d, 3 * Y : 4 * Y, :] = s_ref[px * Y : (px + 1) * Y, :]
        else:
            send[0, d, 3 * X : 4 * X, :] = s_ref[pl.ds(py, X, stride=Y), :]
    launch(0)

    hx, hy = X // 2, Y // 2

    def pieces(d):
        return {1: hy, 6: hy, 3: hx, 4: hx}.get(d, 1)

    def far_copy(d, i):
        source, slot = {
            1: lambda: (panel.at[:, 0, i], far_x.at[1, :, i]),
            3: lambda: (panel.at[:, i, 0], far_y.at[1, :, i]),
            0: lambda: (panel.at[:, 0, 0], far_c.at[1]),
            6: lambda: (image_x.at[:, hy + i], far_x.at[0, :, i]),
            4: lambda: (image_y.at[:, hx + i], far_y.at[0, :, i]),
            5: lambda: (image_c.at[0], far_c.at[0]),
        }[d]()
        return pltpu.make_async_remote_copy(
            src_ref=source, dst_ref=slot, send_sem=far_send.at[d, i], recv_sem=far_recv.at[7 - d, i],
            device_id=peer(d), device_id_type=MESH,
        )

    def far_arrival(d, i):
        buffer, side = {6: (far_x, 1), 4: (far_y, 1), 7: (far_c, 1), 1: (far_x, 0), 3: (far_y, 0), 2: (far_c, 0)}[d]
        here = buffer.at[side] if d in (2, 7) else buffer.at[side, :, i]
        return pltpu.make_async_remote_copy(
            src_ref=here, dst_ref=here, send_sem=far_send.at[d, i], recv_sem=far_recv.at[d, i],
            device_id=peer(d), device_id_type=MESH,
        )

    def far_start(*which):
        for d, i in which:

            @pl.when(exists(d))
            def _():
                far_copy(d, i).start()

    def make_image(d):
        sx, sy = neighbours[d]
        px, py = (0 if sx < 0 else X - 1), (0 if sy < 0 else Y - 1)

        @pl.when(exists(d))
        def _():
            if sx and sy:
                parts = ring_image([panel[c, px, py].reshape(1, K, Z) for c in range(3)], sx, sy)
                for c in range(3):
                    image_c[0 if d == 5 else 1, c] = parts[c].reshape(K, Z)
            else:

                def body(t, carry):
                    group = pl.ds(pl.multiple_of(t * 8, 8), 8)
                    if sx:
                        edge = [panel[c, px, :, group, :] for c in range(3)]
                    else:
                        edge = [panel[c, :, py, group, :] for c in range(3)]
                    parts = ring_image(edge, sx, sy)
                    for c in range(3):
                        if sx:
                            image_x[c, :, group, :] = parts[c]
                        else:
                            image_y[c, :, group, :] = parts[c]
                    return carry

                lax.fori_loop(0, K // 8, body, 0)

    def part_copy(d):
        return pltpu.make_async_remote_copy(
            src_ref=share.at[d], dst_ref=share_far.at[7 - d], send_sem=part_send.at[d], recv_sem=part_recv.at[7 - d],
            device_id=peer(d), device_id_type=MESH,
        )

    def part_arrival(d):
        return pltpu.make_async_remote_copy(
            src_ref=share.at[d], dst_ref=share_far.at[d], send_sem=part_send.at[d], recv_sem=part_recv.at[d],
            device_id=peer(d), device_id_type=MESH,
        )

    def make_part(d):
        @pl.when(exists(d))
        def _():
            for i in range(pieces(d)):
                far_arrival(d, i).wait_recv()
            left, right = [], []
            for c in range(3):
                if d == 6:
                    for y in range(hy):
                        left.append(image_x[c, y])
                        right.append(far_x[1, c, y])
                elif d == 4:
                    for x in range(hx):
                        left.append(image_y[c, x])
                        right.append(far_y[1, c, x])
                elif d == 7:
                    left.append(image_c[1, c])
                    right.append(far_c[1, c])
                elif d == 1:
                    for y in range(hy, Y):
                        left.append(far_x[0, c, y - hy])
                        right.append(panel[c, 0, y])
                elif d == 3:
                    for x in range(hx, X):
                        left.append(far_y[0, c, x - hx])
                        right.append(panel[c, x, 0])
                else:
                    left.append(far_c[0, c])
                    right.append(panel[c, 0, Y - 1])
            acc = lax.dot_general(
                jnp.concatenate([split_rows(v) for v in left], axis=1),
                jnp.concatenate([split_rows(v) for v in right], axis=1),
                (((1,), (1,)), ((), ())),
                preferred_element_type=jnp.float32,
            )
            half = acc[0:K] + acc[K : 2 * K]
            tile = half[:, 0:K] + half[:, K : 2 * K]
            share[d] = jnp.concatenate([tile[0 : K // 2], tile[K // 2 : K]], axis=1)
            part_copy(d).start()

    def together(*groups):
        return [(d, i) for d, low, high in groups for i in range(low, min(high, pieces(d)))]

    quarter = max(hy // 4, 1)
    after = {
        0: together((1, 0, 2 * quarter), (3, 0, hx)),
        1: together((1, 2 * quarter, 3 * quarter), (6, quarter, 2 * quarter), (4, 0, hx)),
        2: together((1, 3 * quarter, hy), (6, 2 * quarter, 3 * quarter)),
        4: together((0, 0, 1), (5, 0, 1), (6, 3 * quarter, hy)),
    }
    far_start(*after[0])
    for d in (6, 4, 5, 7):
        make_image(d)
    far_start(*together((6, 0, quarter)))

    def diagonal(t, carry):
        first = pl.multiple_of(t * 8, 8)

        def at(c, y):
            return panel[c, :, y, pl.ds(first, 8), :]

        total = jnp.zeros((X, 8, Z), jnp.float32)
        for c in range(3):
            sums = [at(c, y) + shift_lead(at(c, y), 1, 0) + shift_lead(at(c, y), -1, 0) for y in range(Y)]
            for y in range(Y):
                v, across = at(c, y), sums[y]
                if y > 0:
                    across = across + sums[y - 1]
                if y < Y - 1:
                    across = across + sums[y + 1]
                scale = jnp.stack(
                    [jnp.broadcast_to(27.0 + s_ref[x * Y + y : x * Y + y + 1, :], (8, Z)) for x in range(X)]
                )
                total = total + v * (scale * v - across) - 2.0 * shift_z(v, 1) * across
        dz2 = [shift_z(at(2, y), 1) - shift_z(at(2, y), -1) for y in range(Y)]
        for y in range(Y):
            both, dy = dz2[y], jnp.zeros((X, 8, Z), jnp.float32)
            if y > 0:
                both, dy = both - at(1, y - 1), dy - dz2[y - 1]
            if y < Y - 1:
                both, dy = both + at(1, y + 1), dy + dz2[y + 1]
            dx = shift_lead(both, 1, 0) - shift_lead(both, -1, 0)
            total = total + 2.0 * mixing * (at(0, y) * dx + at(1, y) * dy)
        part = jnp.sum(total, axis=0)
        whole = jnp.sum(part, axis=1, keepdims=True)
        weight[pl.ds(first, 8), :] = jnp.broadcast_to(damping / whole, (8, Z))
        return carry

    lax.fori_loop(0, K // 8, diagonal, 0)

    def restrict(field):
        def body(y, acc):
            for c in range(3):
                for x in range(X):
                    acc = acc + panel[c, x, y] * field[pl.ds((c * X + x) * Y + y, 1), :]
            return acc

        acc = lax.fori_loop(0, Y, body, jnp.zeros((K, Z), jnp.float32))
        return jnp.broadcast_to(jnp.sum(acc, axis=1, keepdims=True), (K, Z))

    def prolong(vector):
        coarse[...] = vector

        def body(k, acc):
            block = z_ref[pl.ds(pl.multiple_of(k * rows, 8), rows), :].reshape(3 * X, Y, Z)
            return acc + block * coarse[pl.ds(k, 1), :][None]

        acc = lax.fori_loop(0, K, body, jnp.zeros((3 * X, Y, Z), jnp.float32), unroll=4)
        return acc.reshape(rows, Z)

    def put_own(target, field):
        for c in range(3):
            for x in range(X):
                here, there = (c * wide + 2 + x) * 16, (c * X + x) * Y
                target[here : here + Y, :] = field[there : there + Y, :]

    def operate(padded, field):
        out = stencil(padded, wide, 2, X)
        scale = 27.0 + s_ref[...]
        per = X * Y
        return [scale * field[c * per : (c + 1) * per, :] + out[c][:, 0:Y].reshape(per, Z) for c in range(3)]

    def inner(ref, c):
        first = (c * wide + 1) * 16
        return slice(first, first + (X + 2) * 16)

    def apply_both(turn, current, result, image, filler):
        first = weight[...] * restrict(current)
        own_p[...] = prolong(first)
        pack_own(turn + 1, own_p)
        launch(turn + 1)
        far_start(*after.get(turn + 1, ()))
        put_own(ext_r, current)
        put_own(ext_p, own_p)
        await_all(turn)
        unpack_halo(turn, ext_r)
        if turn == 0:
            for x in range(X):
                ext_inv[(2 + x) * 16 : (2 + x) * 16 + Y, :] = s_ref[x * Y : (x + 1) * Y, :]
            for d, (sx, sy) in enumerate(neighbours):
                px, py = (1 if sx < 0 else X + 2), (15 if sy < 0 else 8)
                if sx and sy:
                    ext_inv[px * 16 + py : px * 16 + py + 1, :] = recv[0, d, 3:4, :]
                elif sx:
                    ext_inv[px * 16 : px * 16 + Y, :] = recv[0, d, 3 * Y : 4 * Y, :]
                else:
                    ext_inv[pl.ds(2 * 16 + py, X, stride=16), :] = recv[0, d, 3 * X : 4 * X, :]
            shape = ((X + 2) * 16, Z)
            row = lax.rem(lax.broadcasted_iota(jnp.int32, shape, 0), 16)
            inside = jnp.logical_or(row <= 8, row == 15)
            stiff = ext_inv[16 : (X + 3) * 16, :]
            ext_inv[16 : (X + 3) * 16, :] = jnp.where(inside, damping / (26.0 + stiff), 0.0)
        inv = ext_inv[16 : (X + 3) * 16, :]
        for c in range(3):
            ext[inner(ext, c), :] = inv * ext_r[inner(ext, c), :]
        for _ in range(SWEEPS - 1):
            out = stencil(ext, wide, 1, X + 2)
            new = []
            for c in range(3):
                e = ext[inner(ext, c), :]
                change = ext_r[inner(ext, c), :] - e - out[c].reshape((X + 2) * 16, Z)
                new.append((1.0 - damping) * e + inv * change)
            for c in range(3):
                ext[inner(ext, c), :] = new[c]
        await_all(turn + 1)
        unpack_halo(turn + 1, ext_p)
        coarse_image = operate(ext_p, own_p)
        per = X * Y
        for c in range(3):
            own_u[c * per : (c + 1) * per, :] = current[c * per : (c + 1) * per, :] - coarse_image[c]
        own_p[...] = prolong(first + weight[...] * restrict(own_u))
        for c in range(3):
            for x in range(X):
                here, there = (c * wide + 2 + x) * 16, (c * X + x) * Y
                ext[here : here + Y, :] = ext[here : here + Y, :] + own_p[there : there + Y, :]
        pack_strips(turn + 2)
        launch(turn + 2)
        far_start(*after.get(turn + 2, ()))
        filler()
        await_all(turn + 2)
        add_strips(turn + 2)
        for c in range(3):
            for x in range(X):
                here, there = (c * wide + 2 + x) * 16, (c * X + x) * Y
                result[there : there + Y, :] = ext[here : here + Y, :]
        out = operate(ext, result)
        for c in range(3):
            image[c * per : (c + 1) * per, :] = out[c]

    def fill_parts():
        for d in (6, 4, 7):
            make_part(d)

    apply_both(0, r_ref, own_z, own_w, lambda: None)
    pack_own(3, own_w)
    launch(3)
    apply_both(3, own_w, own_v, own_u, fill_parts)

    pairs = ((r_ref, own_z), (own_z, own_w), (r_ref, own_v), (own_w, own_v), (own_z, own_u), (own_v, own_u))
    for i, (a, b) in enumerate(pairs):
        part = jnp.sum((a[...] * b[...]).reshape(3 * X, 8, Z), axis=0)
        dots[i : i + 1, :] = jnp.sum(part, axis=0, keepdims=True)

    def exchange(axis_pos, me, size, buffer, s_sem, r_sem, filler):
        def target(o):
            other = lax.rem(me + o, size)
            return (other, (other, gy) if axis_pos == 0 else (gx, other))

        def copy(o, slot):
            other, where = target(o)
            return pltpu.make_async_remote_copy(
                src_ref=dots,
                dst_ref=buffer.at[me if slot is None else other],
                send_sem=s_sem.at[o],
                recv_sem=r_sem.at[me if slot is None else other],
                device_id=where,
                device_id_type=MESH,
            )

        for o in range(1, size):
            copy(o, None).start()
        buffer[me] = dots[...]
        filler()
        for o in range(1, size):
            copy(o, 1).wait_recv()
        for o in range(1, size):
            copy(o, None).wait_send()
        dots[...] = jnp.sum(buffer[...], axis=0)

    def later_parts():
        for d in (1, 3, 2):
            make_part(d)

    def finish(d):
        @pl.when(exists(d))
        def _():
            whole = share[d] if d in (2, 7) else None
            if d not in (2, 7):
                part_arrival(d).wait_recv()
                whole = share_far[d] if d in (0, 5) else share[d] + share_far[d]
            tile = jnp.concatenate([whole[:, 0:K], whole[:, K : 2 * K]], axis=0)
            square[:, 0:K] = tile if d >= 4 else tile.T
            even = square[pl.ds(0, K // 2, stride=2), :]
            odd = square[pl.ds(1, K // 2, stride=2), :]
            packed[d * K // 2 : (d + 1) * K // 2, :] = jnp.concatenate([even[:, 0:K], odd[:, 0:K]], axis=1)

        @pl.when(jnp.logical_not(exists(d)))
        def _():
            packed[d * K // 2 : (d + 1) * K // 2, :] = jnp.zeros((K // 2, 2 * K), jnp.float32)

    def early_tiles():
        for d in (7, 2):
            finish(d)

    exchange(0, gx, n_gx, sums_x, sx_send, sx_recv, later_parts)
    exchange(1, gy, n_gy, sums_y, sy_send, sy_recv, early_tiles)
    total = jnp.sum(dots[...], axis=1, keepdims=True)
    rz, zw, rv, wv, zu, vu = (total[i : i + 1, :] for i in range(6))
    step0 = rz / zw
    rz_new = step0 * (step0 * wv - rv)
    grow = 1.0 + rz_new / rz
    step1 = rz_new / (grow * grow * zw - grow * step0 * (wv + zu) + step0 * step0 * vu)
    keep = step0 + step1 * grow
    cross = step1 * step0
    x_out[...] = keep * own_z[...] - cross * own_v[...]
    res_out[...] = r_ref[...] - keep * own_w[...] + cross * own_u[...]
    for d in (0, 5, 4, 6, 3, 1):
        finish(d)
    for j in range(K // 2):
        tile_out[:, j * 2 * K : (j + 1) * 2 * K] = packed[pl.ds(j, 8, stride=K // 2), :]

    for d in range(8):

        @pl.when(exists(d))
        def _():
            if d not in (2, 7):
                for i in range(pieces(d)):
                    far_copy(d, i).wait_send()
            if d not in (0, 5):
                part_copy(d).wait_send()
            for turn in range(ROUNDS):
                message(turn, d).wait_send()


def emit(*refs):
    sems = refs[6]
    copies = [pltpu.make_async_copy(refs[i], refs[3 + i], sems.at[i]) for i in range(3)]
    for copy in copies:
        copy.start()
    for copy in copies:
        copy.wait()


def per_device(n_gx, n_gy, right_side, stiffness, panels):
    X, Y, Z = stiffness.shape
    K = panels.shape[0]
    f32 = jnp.float32
    cells = 3 * X * Y
    field = pltpu.VMEM((cells, Z), f32)
    padded = pltpu.VMEM((3 * (X + 4) * 16, Z), f32)
    dma = pltpu.SemaphoreType.DMA
    vmem = pl.BlockSpec(memory_space=pltpu.VMEM)
    anywhere = pl.BlockSpec(memory_space=pltpu.HBM)
    results = (
        jax.ShapeDtypeStruct((cells, Z), f32),
        jax.ShapeDtypeStruct((cells, Z), f32),
        jax.ShapeDtypeStruct((8, K * K), f32),
    )
    values = pl.pallas_call(
        functools.partial(kernel, n_gx, n_gy),
        out_shape=results,
        in_specs=[anywhere] * 3,
        out_specs=(vmem,) * 3,
        scratch_shapes=[
            field,
            pltpu.VMEM((X * Y, Z), f32),
            pltpu.VMEM((K * cells, Z), f32),
            pltpu.VMEM((3, X, Y, K, Z), f32),
            pltpu.VMEM((2, 3, Y // 2, K, Z), f32),
            pltpu.VMEM((2, 3, X // 2, K, Z), f32),
            pltpu.VMEM((2, 3, K, Z), f32),
            pltpu.VMEM((3, Y, K, Z), f32),
            pltpu.VMEM((3, X, K, Z), f32),
            pltpu.VMEM((2, 3, K, Z), f32),
            pltpu.VMEM((8, K // 2, 2 * K), f32),
            pltpu.VMEM((8, K // 2, 2 * K), f32),
            pltpu.VMEM((ROUNDS, 8, 64, Z), f32),
            pltpu.VMEM((ROUNDS, 8, 64, Z), f32),
            padded, padded, padded,
            pltpu.VMEM(((X + 4) * 16, Z), f32),
            field, field, field, field, field,
            pltpu.VMEM((K, Z), f32),
            pltpu.VMEM((K, Z), f32),
            pltpu.VMEM((K, 2 * K), f32),
            pltpu.VMEM((8 * K // 2, 2 * K), f32),
            pltpu.VMEM((8, Z), f32),
            pltpu.VMEM((n_gx, 8, Z), f32),
            pltpu.VMEM((n_gy, 8, Z), f32),
            dma((3,)), dma((ROUNDS, 8)), dma((ROUNDS, 8)), dma((8, Y)), dma((8, Y)), dma((8,)), dma((8,)),
            dma((n_gx,)), dma((n_gx,)), dma((n_gy,)), dma((n_gy,)),
        ],
        compiler_params=pltpu.CompilerParams(
            collective_id=0, has_side_effects=True, vmem_limit_bytes=56 * 1024 * 1024
        ),
    )(right_side.reshape(cells, Z), stiffness.reshape(X * Y, Z), panels.reshape(K * cells, Z))
    x, res, tiles = pl.pallas_call(
        emit,
        out_shape=results,
        in_specs=[anywhere] * 3,
        out_specs=(vmem,) * 3,
        scratch_shapes=[dma((3,))],
        compiler_params=pltpu.CompilerParams(vmem_limit_bytes=63 * 1024 * 1024),
    )(*values)
    return x.reshape(3, X, Y, Z), res.reshape(3, X, Y, Z), tiles.reshape(1, 1, 8, K * K)


def solution(mesh):
    n_gx, n_gy = mesh.shape["gx"], mesh.shape["gy"]
    return jax.shard_map(
        functools.partial(per_device, n_gx, n_gy),
        mesh=mesh,
        in_specs=(P(None, "gx", "gy", None), P("gx", "gy", None), P(None, None, "gx", "gy", None)),
        out_specs=(P(None, "gx", "gy", None), P(None, "gx", "gy", None), P("gx", "gy", None, None)),
        check_vma=False,
    )
```

```python
import functools

import jax
import jax.numpy as jnp
from jax import lax
from jax.experimental import pallas as pl
from jax.experimental.pallas import tpu as pltpu
from jax.sharding import PartitionSpec as P

SWEEPS = 4
MESH = pl.DeviceIdType.MESH
mixing = 0.25
damping = 0.5
neighbours = ((-1, -1), (-1, 0), (-1, 1), (0, -1), (0, 1), (1, -1), (1, 0), (1, 1))
ROUNDS = 6
STRIPS = (2, 5)


def shift_z(value, step):
    axis = value.ndim - 1
    size = value.shape[axis]
    rolled = pltpu.roll(value, (-step) % size, axis)
    lane = lax.broadcasted_iota(jnp.int32, value.shape, axis)
    edge = size - 1 if step == 1 else 0
    return jnp.where(lane == edge, 0.0, rolled)


def shift_lead(value, step, axis):
    size = value.shape[axis]
    zero = jnp.zeros_like(lax.slice_in_dim(value, 0, 1, axis=axis))
    if step == 1:
        return jnp.concatenate([lax.slice_in_dim(value, 1, size, axis=axis), zero], axis=axis)
    return jnp.concatenate([zero, lax.slice_in_dim(value, 0, size - 1, axis=axis)], axis=axis)


def stencil(field, wide, start, count):
    def planes(c, step):
        first = (c * wide + start + step) * 16
        return field[first : first + count * 16, :].reshape(count, 16, field.shape[1])

    def up(v):
        return pltpu.roll(v, 15, 1)

    def down(v):
        return pltpu.roll(v, 1, 1)

    low = [planes(c, -1) for c in range(3)]
    mid = [planes(c, 0) for c in range(3)]
    high = [planes(c, 1) for c in range(3)]
    box = []
    for c in range(3):
        along = low[c] + mid[c] + high[c]
        box.append(along + up(along) + down(along))
    dx0, dx1, dx2 = (high[c] - low[c] for c in range(3))
    dy1 = up(mid[1]) - down(mid[1])
    dz2 = shift_z(mid[2], 1) - shift_z(mid[2], -1)
    side0 = mixing * dx2
    out0 = (
        mixing * (up(dx1) - down(dx1)) - box[0] + shift_z(side0 - box[0], 1) - shift_z(side0 + box[0], -1)
    )
    side1 = mixing * (dx0 + dz2)
    out1 = up(side1) - down(side1) - box[1] - shift_z(box[1], 1) - shift_z(box[1], -1)
    side2 = mixing * (dx0 + dy1)
    out2 = shift_z(side2 - box[2], 1) - shift_z(side2 + box[2], -1) - box[2]
    return out0, out1, out2


def ring_image(edge, sx, sy):
    boxes = []
    for c in range(3):
        v = edge[c]
        if sx == 0 or sy == 0:
            v = v + shift_lead(v, 1, 0) + shift_lead(v, -1, 0)
        boxes.append(v + shift_z(v, 1) + shift_z(v, -1))
    if sx and sy:
        return [mixing * sx * sy * edge[1] - boxes[0], mixing * sx * sy * edge[0] - boxes[1], -boxes[2]]

    def along(v):
        return shift_lead(v, 1, 0) - shift_lead(v, -1, 0)

    def third(v):
        return shift_z(v, 1) - shift_z(v, -1)

    if sx:
        return [
            -mixing * sx * (along(edge[1]) + third(edge[2])) - boxes[0],
            -mixing * sx * along(edge[0]) - boxes[1],
            -mixing * sx * third(edge[0]) - boxes[2],
        ]
    return [
        -mixing * sy * along(edge[1]) - boxes[0],
        -mixing * sy * (along(edge[0]) + third(edge[2])) - boxes[1],
        -mixing * sy * third(edge[1]) - boxes[2],
    ]


def split_rows(value):
    high = value.astype(jnp.bfloat16)
    low = (value - high.astype(jnp.float32)).astype(jnp.bfloat16)
    return jnp.concatenate([high, low], axis=0)


def kernel(
    n_gx, n_gy, r_hbm, s_hbm, z_hbm, x_out, res_out, tile_out,
    r_ref, s_ref, z_ref, panel, far_x, far_y, far_c, image_x, image_y, image_c, share, share_far, send, recv, ext, ext_r, ext_p, ext_inv, own_p, own_z, own_w, own_v, own_u,
    weight, coarse, square, packed, dots, sums_x, sums_y,
    in_sem, send_sem, recv_sem, far_send, far_recv, part_send, part_recv, sx_send, sx_recv, sy_send, sy_recv,
):
    X, Y, K, Z = panel.shape[1:]
    wide = X + 4
    rows = 3 * X * Y
    gx, gy = lax.axis_index("gx"), lax.axis_index("gy")

    def exists(d):
        sx, sy = neighbours[d]
        ok = jnp.bool_(True)
        if sx < 0:
            ok = gx > 0
        if sx > 0:
            ok = gx < n_gx - 1
        if sy:
            ok_y = gy > 0 if sy < 0 else gy < n_gy - 1
            ok = jnp.logical_and(ok, ok_y) if sx else ok_y
        return ok

    def peer(d):
        return (gx + neighbours[d][0], gy + neighbours[d][1])

    load_z = pltpu.make_async_copy(z_hbm, z_ref, in_sem.at[0])
    load_r = pltpu.make_async_copy(r_hbm, r_ref, in_sem.at[1])
    load_s = pltpu.make_async_copy(s_hbm, s_ref, in_sem.at[2])
    load_r.start()
    load_s.start()
    load_z.start()
    recv[...] = jnp.zeros_like(recv)
    barrier = pltpu.get_barrier_semaphore()
    count = jnp.int32(n_gx - 1 + n_gy - 1)
    for o in range(1, n_gx):
        pl.semaphore_signal(barrier, inc=1, device_id=(lax.rem(gx + o, n_gx), gy), device_id_type=MESH)
    for o in range(1, n_gy):
        pl.semaphore_signal(barrier, inc=1, device_id=(gx, lax.rem(gy + o, n_gy)), device_id_type=MESH)
    for d in (0, 2, 5, 7):
        count = count + exists(d).astype(jnp.int32)

        @pl.when(exists(d))
        def _():
            pl.semaphore_signal(barrier, inc=1, device_id=peer(d), device_id_type=MESH)

    ext[...] = jnp.zeros_like(ext)
    ext_r[...] = jnp.zeros_like(ext_r)
    ext_p[...] = jnp.zeros_like(ext_p)
    ext_inv[...] = jnp.zeros_like(ext_inv)
    dots[...] = jnp.zeros_like(dots)
    load_r.wait()
    load_s.wait()

    def relayout(y, carry):
        for c in range(3):
            for x in range(X):
                for t in range(K // 8):
                    row = (c * X + x) * Y + y + t * 8 * rows
                    panel[c, x, y, t * 8 : t * 8 + 8, :] = z_ref[pl.ds(row, 8, stride=rows), :]
        return carry

    load_z.wait()
    lax.fori_loop(0, Y, relayout, 0)

    pl.semaphore_wait(barrier, count)

    def length(turn, d):
        sx, sy = neighbours[d]
        if turn in STRIPS:
            return 16 if sx and sy else (64 if sx else 48)
        if sx and sy:
            return 8
        if sx:
            return 32 if turn == 0 else 24
        return 16

    def message(turn, d):
        n = length(turn, d)
        return pltpu.make_async_remote_copy(
            src_ref=send.at[turn, d, 0:n],
            dst_ref=recv.at[turn, 7 - d, 0:n],
            send_sem=send_sem.at[turn, d],
            recv_sem=recv_sem.at[turn, 7 - d],
            device_id=peer(d),
            device_id_type=MESH,
        )

    def arrival(turn, d):
        n = length(turn, d)
        return pltpu.make_async_remote_copy(
            src_ref=send.at[turn, d, 0:n],
            dst_ref=recv.at[turn, d, 0:n],
            send_sem=send_sem.at[turn, d],
            recv_sem=recv_sem.at[turn, d],
            device_id=peer(d),
            device_id_type=MESH,
        )

    def launch(turn):
        for d in range(8):

            @pl.when(exists(d))
            def _():
                message(turn, d).start()

    def await_all(turn):
        for d in range(8):

            @pl.when(exists(d))
            def _():
                arrival(turn, d).wait_recv()

    def pack_own(turn, field):
        for d, (sx, sy) in enumerate(neighbours):
            px, py = (0 if sx < 0 else X - 1), (0 if sy < 0 else Y - 1)
            if sx and sy:
                send[turn, d, 0:3, :] = field[pl.ds(px * Y + py, 3, stride=X * Y), :]
                continue
            for c in range(3):
                if sx:
                    first = (c * X + px) * Y
                    send[turn, d, c * Y : (c + 1) * Y, :] = field[first : first + Y, :]
                else:
                    send[turn, d, c * X : (c + 1) * X, :] = field[pl.ds(c * X * Y + py, X, stride=Y), :]

    def unpack_halo(turn, target):
        for d, (sx, sy) in enumerate(neighbours):
            px, py = (1 if sx < 0 else X + 2), (15 if sy < 0 else 8)
            if sx and sy:
                target[pl.ds(px * 16 + py, 3, stride=wide * 16), :] = recv[turn, d, 0:3, :]
                continue
            for c in range(3):
                if sx:
                    first = (c * wide + px) * 16
                    target[first : first + Y, :] = recv[turn, d, c * Y : (c + 1) * Y, :]
                else:
                    first = (c * wide + 2) * 16 + py
                    target[pl.ds(first, X, stride=16), :] = recv[turn, d, c * X : (c + 1) * X, :]

    def strips(turn, visit):
        for d, (sx, sy) in enumerate(neighbours):
            p0, ys = (1 if sx < 0 else X + 1), ((15, 0) if sy < 0 else (7, 8))
            if sx == 0:
                for c in range(3):
                    for t in range(2):
                        first = (c * 2 + t) * 8
                        visit(d, pl.ds((c * wide + 1) * 16 + ys[t], X + 2, stride=16), slice(first, first + X + 2))
                continue
            if sy == 0:
                for c in range(3):
                    for p in range(2):
                        first, row = (c * 2 + p) * 8, (c * wide + p0 + p) * 16
                        visit(d, slice(row, row + 8), slice(first, first + 8))
                ys = (15, 8)
            base = 48 if sy == 0 else 0
            for p in range(2):
                for t in range(2):
                    first = base + (p * 2 + t) * 4
                    visit(d, pl.ds((p0 + p) * 16 + ys[t], 3, stride=wide * 16), slice(first, first + 3))

    def pack_strips(turn):
        def visit(d, here, there):
            send[turn, d, there, :] = ext[here, :]

        strips(turn, visit)

    def add_strips(turn):
        def visit(d, here, there):
            ext[here, :] = ext[here, :] + recv[turn, d, there, :]

        strips(turn, visit)
        for ok, plane in ((gx == 0, 1), (gx == n_gx - 1, X + 2)):

            @pl.when(ok)
            def _():
                for c in range(3):
                    first = (c * wide + plane) * 16
                    ext[first : first + 16, :] = jnp.zeros((16, Z), jnp.float32)

        for ok, row in ((gy == 0, 15), (gy == n_gy - 1, 8)):

            @pl.when(ok)
            def _():
                for c in range(3):
                    first = (c * wide + 1) * 16 + row
                    ext[pl.ds(first, X + 2, stride=16), :] = jnp.zeros((X + 2, Z), jnp.float32)

    pack_own(0, r_ref)
    for d, (sx, sy) in enumerate(neighbours):
        px, py = (0 if sx < 0 else X - 1), (0 if sy < 0 else Y - 1)
        if sx and sy:
            send[0, d, 3:4, :] = s_ref[px * Y + py : px * Y + py + 1, :]
        elif sx:
            send[0, d, 3 * Y : 4 * Y, :] = s_ref[px * Y : (px + 1) * Y, :]
        else:
            send[0, d, 3 * X : 4 * X, :] = s_ref[pl.ds(py, X, stride=Y), :]
    launch(0)

    hx, hy = X // 2, Y // 2

    def pieces(d):
        return {1: hy, 6: hy, 3: hx, 4: hx}.get(d, 1)

    def far_copy(d, i):
        source, slot = {
            1: lambda: (panel.at[:, 0, i], far_x.at[1, :, i]),
            3: lambda: (panel.at[:, i, 0], far_y.at[1, :, i]),
            0: lambda: (panel.at[:, 0, 0], far_c.at[1]),
            6: lambda: (image_x.at[:, hy + i], far_x.at[0, :, i]),
            4: lambda: (image_y.at[:, hx + i], far_y.at[0, :, i]),
            5: lambda: (image_c.at[0], far_c.at[0]),
        }[d]()
        return pltpu.make_async_remote_copy(
            src_ref=source, dst_ref=slot, send_sem=far_send.at[d, i], recv_sem=far_recv.at[7 - d, i],
            device_id=peer(d), device_id_type=MESH,
        )

    def far_arrival(d, i):
        buffer, side = {6: (far_x, 1), 4: (far_y, 1), 7: (far_c, 1), 1: (far_x, 0), 3: (far_y, 0), 2: (far_c, 0)}[d]
        here = buffer.at[side] if d in (2, 7) else buffer.at[side, :, i]
        return pltpu.make_async_remote_copy(
            src_ref=here, dst_ref=here, send_sem=far_send.at[d, i], recv_sem=far_recv.at[d, i],
            device_id=peer(d), device_id_type=MESH,
        )

    def far_start(*which):
        for d, i in which:

            @pl.when(exists(d))
            def _():
                far_copy(d, i).start()

    def make_image(d):
        sx, sy = neighbours[d]
        px, py = (0 if sx < 0 else X - 1), (0 if sy < 0 else Y - 1)

        @pl.when(exists(d))
        def _():
            if sx and sy:
                parts = ring_image([panel[c, px, py].reshape(1, K, Z) for c in range(3)], sx, sy)
                for c in range(3):
                    image_c[0 if d == 5 else 1, c] = parts[c].reshape(K, Z)
            else:

                def body(t, carry):
                    group = pl.ds(pl.multiple_of(t * 8, 8), 8)
                    if sx:
                        edge = [panel[c, px, :, group, :] for c in range(3)]
                    else:
                        edge = [panel[c, :, py, group, :] for c in range(3)]
                    parts = ring_image(edge, sx, sy)
                    for c in range(3):
                        if sx:
                            image_x[c, :, group, :] = parts[c]
                        else:
                            image_y[c, :, group, :] = parts[c]
                    return carry

                lax.fori_loop(0, K // 8, body, 0)

    def part_copy(d):
        return pltpu.make_async_remote_copy(
            src_ref=share.at[d], dst_ref=share_far.at[7 - d], send_sem=part_send.at[d], recv_sem=part_recv.at[7 - d],
            device_id=peer(d), device_id_type=MESH,
        )

    def part_arrival(d):
        return pltpu.make_async_remote_copy(
            src_ref=share.at[d], dst_ref=share_far.at[d], send_sem=part_send.at[d], recv_sem=part_recv.at[d],
            device_id=peer(d), device_id_type=MESH,
        )

    def make_part(d):
        @pl.when(exists(d))
        def _():
            for i in range(pieces(d)):
                far_arrival(d, i).wait_recv()
            left, right = [], []
            for c in range(3):
                if d == 6:
                    for y in range(hy):
                        left.append(image_x[c, y])
                        right.append(far_x[1, c, y])
                elif d == 4:
                    for x in range(hx):
                        left.append(image_y[c, x])
                        right.append(far_y[1, c, x])
                elif d == 7:
                    left.append(image_c[1, c])
                    right.append(far_c[1, c])
                elif d == 1:
                    for y in range(hy, Y):
                        left.append(far_x[0, c, y - hy])
                        right.append(panel[c, 0, y])
                elif d == 3:
                    for x in range(hx, X):
                        left.append(far_y[0, c, x - hx])
                        right.append(panel[c, x, 0])
                else:
                    left.append(far_c[0, c])
                    right.append(panel[c, 0, Y - 1])
            acc = lax.dot_general(
                jnp.concatenate([split_rows(v) for v in left], axis=1),
                jnp.concatenate([split_rows(v) for v in right], axis=1),
                (((1,), (1,)), ((), ())),
                preferred_element_type=jnp.float32,
            )
            half = acc[0:K] + acc[K : 2 * K]
            tile = half[:, 0:K] + half[:, K : 2 * K]
            share[d] = jnp.concatenate([tile[0 : K // 2], tile[K // 2 : K]], axis=1)
            part_copy(d).start()

    def together(*groups):
        return [(d, i) for d, low, high in groups for i in range(low, min(high, pieces(d)))]

    quarter = max(hy // 4, 1)
    after = {
        0: together((1, 0, 2 * quarter), (3, 0, hx)),
        1: together((1, 2 * quarter, 3 * quarter), (6, quarter, 2 * quarter), (4, 0, hx)),
        2: together((1, 3 * quarter, hy), (6, 2 * quarter, 3 * quarter)),
        4: together((0, 0, 1), (5, 0, 1), (6, 3 * quarter, hy)),
    }
    far_start(*after[0])
    for d in (6, 4, 5, 7):
        make_image(d)
    far_start(*together((6, 0, quarter)))

    def diagonal(t, carry):
        first = pl.multiple_of(t * 8, 8)

        def at(c, y):
            return panel[c, :, y, pl.ds(first, 8), :]

        total = jnp.zeros((X, 8, Z), jnp.float32)
        for c in range(3):
            sums = [at(c, y) + shift_lead(at(c, y), 1, 0) + shift_lead(at(c, y), -1, 0) for y in range(Y)]
            for y in range(Y):
                v, across = at(c, y), sums[y]
                if y > 0:
                    across = across + sums[y - 1]
                if y < Y - 1:
                    across = across + sums[y + 1]
                scale = jnp.stack(
                    [jnp.broadcast_to(27.0 + s_ref[x * Y + y : x * Y + y + 1, :], (8, Z)) for x in range(X)]
                )
                total = total + v * (scale * v - across) - 2.0 * shift_z(v, 1) * across
        dz2 = [shift_z(at(2, y), 1) - shift_z(at(2, y), -1) for y in range(Y)]
        for y in range(Y):
            both, dy = dz2[y], jnp.zeros((X, 8, Z), jnp.float32)
            if y > 0:
                both, dy = both - at(1, y - 1), dy - dz2[y - 1]
            if y < Y - 1:
                both, dy = both + at(1, y + 1), dy + dz2[y + 1]
            dx = shift_lead(both, 1, 0) - shift_lead(both, -1, 0)
            total = total + 2.0 * mixing * (at(0, y) * dx + at(1, y) * dy)
        part = jnp.sum(total, axis=0)
        whole = jnp.sum(part, axis=1, keepdims=True)
        weight[pl.ds(first, 8), :] = jnp.broadcast_to(damping / whole, (8, Z))
        return carry

    lax.fori_loop(0, K // 8, diagonal, 0)

    def restrict(field):
        def body(y, acc):
            for c in range(3):
                for x in range(X):
                    acc = acc + panel[c, x, y] * field[pl.ds((c * X + x) * Y + y, 1), :]
            return acc

        acc = lax.fori_loop(0, Y, body, jnp.zeros((K, Z), jnp.float32))
        return jnp.broadcast_to(jnp.sum(acc, axis=1, keepdims=True), (K, Z))

    def prolong(vector):
        coarse[...] = vector

        def body(k, acc):
            block = z_ref[pl.ds(pl.multiple_of(k * rows, 8), rows), :].reshape(3 * X, Y, Z)
            return acc + block * coarse[pl.ds(k, 1), :][None]

        acc = lax.fori_loop(0, K, body, jnp.zeros((3 * X, Y, Z), jnp.float32), unroll=4)
        return acc.reshape(rows, Z)

    def put_own(target, field):
        for c in range(3):
            for x in range(X):
                here, there = (c * wide + 2 + x) * 16, (c * X + x) * Y
                target[here : here + Y, :] = field[there : there + Y, :]

    def operate(padded, field):
        out = stencil(padded, wide, 2, X)
        scale = 27.0 + s_ref[...]
        per = X * Y
        return [scale * field[c * per : (c + 1) * per, :] + out[c][:, 0:Y].reshape(per, Z) for c in range(3)]

    def inner(ref, c):
        first = (c * wide + 1) * 16
        return slice(first, first + (X + 2) * 16)

    def apply_both(turn, current, result, image, filler):
        first = weight[...] * restrict(current)
        own_p[...] = prolong(first)
        pack_own(turn + 1, own_p)
        launch(turn + 1)
        far_start(*after.get(turn + 1, ()))
        put_own(ext_r, current)
        put_own(ext_p, own_p)
        await_all(turn)
        unpack_halo(turn, ext_r)
        if turn == 0:
            for x in range(X):
                ext_inv[(2 + x) * 16 : (2 + x) * 16 + Y, :] = s_ref[x * Y : (x + 1) * Y, :]
            for d, (sx, sy) in enumerate(neighbours):
                px, py = (1 if sx < 0 else X + 2), (15 if sy < 0 else 8)
                if sx and sy:
                    ext_inv[px * 16 + py : px * 16 + py + 1, :] = recv[0, d, 3:4, :]
                elif sx:
                    ext_inv[px * 16 : px * 16 + Y, :] = recv[0, d, 3 * Y : 4 * Y, :]
                else:
                    ext_inv[pl.ds(2 * 16 + py, X, stride=16), :] = recv[0, d, 3 * X : 4 * X, :]
            shape = ((X + 2) * 16, Z)
            row = lax.rem(lax.broadcasted_iota(jnp.int32, shape, 0), 16)
            inside = jnp.logical_or(row <= 8, row == 15)
            stiff = ext_inv[16 : (X + 3) * 16, :]
            ext_inv[16 : (X + 3) * 16, :] = jnp.where(inside, damping / (26.0 + stiff), 0.0)
        inv = ext_inv[16 : (X + 3) * 16, :]
        for c in range(3):
            ext[inner(ext, c), :] = inv * ext_r[inner(ext, c), :]
        for _ in range(SWEEPS - 1):
            out = stencil(ext, wide, 1, X + 2)
            new = []
            for c in range(3):
                e = ext[inner(ext, c), :]
                change = ext_r[inner(ext, c), :] - e - out[c].reshape((X + 2) * 16, Z)
                new.append((1.0 - damping) * e + inv * change)
            for c in range(3):
                ext[inner(ext, c), :] = new[c]
        await_all(turn + 1)
        unpack_halo(turn + 1, ext_p)
        coarse_image = operate(ext_p, own_p)
        per = X * Y
        for c in range(3):
            own_u[c * per : (c + 1) * per, :] = current[c * per : (c + 1) * per, :] - coarse_image[c]
        own_p[...] = prolong(first + weight[...] * restrict(own_u))
        for c in range(3):
            for x in range(X):
                here, there = (c * wide + 2 + x) * 16, (c * X + x) * Y
                ext[here : here + Y, :] = ext[here : here + Y, :] + own_p[there : there + Y, :]
        pack_strips(turn + 2)
        launch(turn + 2)
        far_start(*after.get(turn + 2, ()))
        filler()
        await_all(turn + 2)
        add_strips(turn + 2)
        for c in range(3):
            for x in range(X):
                here, there = (c * wide + 2 + x) * 16, (c * X + x) * Y
                result[there : there + Y, :] = ext[here : here + Y, :]
        out = operate(ext, result)
        for c in range(3):
            image[c * per : (c + 1) * per, :] = out[c]

    def parts_of(*which):
        def fill():
            for d in which:
                make_part(d)

        return fill

    apply_both(0, r_ref, own_z, own_w, parts_of(4, 3))
    pack_own(3, own_w)
    launch(3)
    apply_both(3, own_w, own_v, own_u, parts_of(6, 7))

    pairs = ((r_ref, own_z), (own_z, own_w), (r_ref, own_v), (own_w, own_v), (own_z, own_u), (own_v, own_u))
    for i, (a, b) in enumerate(pairs):
        part = jnp.sum((a[...] * b[...]).reshape(3 * X, 8, Z), axis=0)
        dots[i : i + 1, :] = jnp.sum(part, axis=0, keepdims=True)

    def exchange(axis_pos, me, size, buffer, s_sem, r_sem, filler):
        def target(o):
            other = lax.rem(me + o, size)
            return (other, (other, gy) if axis_pos == 0 else (gx, other))

        def copy(o, slot):
            other, where = target(o)
            return pltpu.make_async_remote_copy(
                src_ref=dots,
                dst_ref=buffer.at[me if slot is None else other],
                send_sem=s_sem.at[o],
                recv_sem=r_sem.at[me if slot is None else other],
                device_id=where,
                device_id_type=MESH,
            )

        for o in range(1, size):
            copy(o, None).start()
        buffer[me] = dots[...]
        filler()
        for o in range(1, size):
            copy(o, 1).wait_recv()
        for o in range(1, size):
            copy(o, None).wait_send()
        dots[...] = jnp.sum(buffer[...], axis=0)

    def finish(d):
        @pl.when(exists(d))
        def _():
            whole = share[d] if d in (2, 7) else None
            if d not in (2, 7):
                part_arrival(d).wait_recv()
                whole = share_far[d] if d in (0, 5) else share[d] + share_far[d]
            tile = jnp.concatenate([whole[:, 0:K], whole[:, K : 2 * K]], axis=0)
            square[:, 0:K] = tile if d >= 4 else tile.T
            even = square[pl.ds(0, K // 2, stride=2), :]
            odd = square[pl.ds(1, K // 2, stride=2), :]
            packed[d * K // 2 : (d + 1) * K // 2, :] = jnp.concatenate([even[:, 0:K], odd[:, 0:K]], axis=1)

        @pl.when(jnp.logical_not(exists(d)))
        def _():
            packed[d * K // 2 : (d + 1) * K // 2, :] = jnp.zeros((K // 2, 2 * K), jnp.float32)

    def early_tiles():
        for d in (7, 2, 0, 4, 3):
            finish(d)

    exchange(0, gx, n_gx, sums_x, sx_send, sx_recv, parts_of(1, 2))
    exchange(1, gy, n_gy, sums_y, sy_send, sy_recv, early_tiles)
    total = jnp.sum(dots[...], axis=1, keepdims=True)
    rz, zw, rv, wv, zu, vu = (total[i : i + 1, :] for i in range(6))
    step0 = rz / zw
    rz_new = step0 * (step0 * wv - rv)
    grow = 1.0 + rz_new / rz
    step1 = rz_new / (grow * grow * zw - grow * step0 * (wv + zu) + step0 * step0 * vu)
    keep = step0 + step1 * grow
    cross = step1 * step0
    x_out[...] = keep * own_z[...] - cross * own_v[...]
    res_out[...] = r_ref[...] - keep * own_w[...] + cross * own_u[...]
    for d in (5, 6, 1):
        finish(d)
    for j in range(K // 2):
        tile_out[:, j * 2 * K : (j + 1) * 2 * K] = packed[pl.ds(j, 8, stride=K // 2), :]

    for d in range(8):

        @pl.when(exists(d))
        def _():
            if d not in (2, 7):
                for i in range(pieces(d)):
                    far_copy(d, i).wait_send()
            if d not in (0, 5):
                part_copy(d).wait_send()
            for turn in range(ROUNDS):
                message(turn, d).wait_send()


def emit(*refs):
    sems = refs[6]
    copies = [pltpu.make_async_copy(refs[i], refs[3 + i], sems.at[i]) for i in range(3)]
    for copy in copies:
        copy.start()
    for copy in copies:
        copy.wait()


def per_device(n_gx, n_gy, right_side, stiffness, panels):
    X, Y, Z = stiffness.shape
    K = panels.shape[0]
    f32 = jnp.float32
    cells = 3 * X * Y
    field = pltpu.VMEM((cells, Z), f32)
    padded = pltpu.VMEM((3 * (X + 4) * 16, Z), f32)
    dma = pltpu.SemaphoreType.DMA
    vmem = pl.BlockSpec(memory_space=pltpu.VMEM)
    anywhere = pl.BlockSpec(memory_space=pltpu.HBM)
    results = (
        jax.ShapeDtypeStruct((cells, Z), f32),
        jax.ShapeDtypeStruct((cells, Z), f32),
        jax.ShapeDtypeStruct((8, K * K), f32),
    )
    values = pl.pallas_call(
        functools.partial(kernel, n_gx, n_gy),
        out_shape=results,
        in_specs=[anywhere] * 3,
        out_specs=(vmem,) * 3,
        scratch_shapes=[
            field,
            pltpu.VMEM((X * Y, Z), f32),
            pltpu.VMEM((K * cells, Z), f32),
            pltpu.VMEM((3, X, Y, K, Z), f32),
            pltpu.VMEM((2, 3, Y // 2, K, Z), f32),
            pltpu.VMEM((2, 3, X // 2, K, Z), f32),
            pltpu.VMEM((2, 3, K, Z), f32),
            pltpu.VMEM((3, Y, K, Z), f32),
            pltpu.VMEM((3, X, K, Z), f32),
            pltpu.VMEM((2, 3, K, Z), f32),
            pltpu.VMEM((8, K // 2, 2 * K), f32),
            pltpu.VMEM((8, K // 2, 2 * K), f32),
            pltpu.VMEM((ROUNDS, 8, 64, Z), f32),
            pltpu.VMEM((ROUNDS, 8, 64, Z), f32),
            padded, padded, padded,
            pltpu.VMEM(((X + 4) * 16, Z), f32),
            field, field, field, field, field,
            pltpu.VMEM((K, Z), f32),
            pltpu.VMEM((K, Z), f32),
            pltpu.VMEM((K, 2 * K), f32),
            pltpu.VMEM((8 * K // 2, 2 * K), f32),
            pltpu.VMEM((8, Z), f32),
            pltpu.VMEM((n_gx, 8, Z), f32),
            pltpu.VMEM((n_gy, 8, Z), f32),
            dma((3,)), dma((ROUNDS, 8)), dma((ROUNDS, 8)), dma((8, Y)), dma((8, Y)), dma((8,)), dma((8,)),
            dma((n_gx,)), dma((n_gx,)), dma((n_gy,)), dma((n_gy,)),
        ],
        compiler_params=pltpu.CompilerParams(
            collective_id=0, has_side_effects=True, vmem_limit_bytes=56 * 1024 * 1024
        ),
    )(right_side.reshape(cells, Z), stiffness.reshape(X * Y, Z), panels.reshape(K * cells, Z))
    x, res, tiles = pl.pallas_call(
        emit,
        out_shape=results,
        in_specs=[anywhere] * 3,
        out_specs=(vmem,) * 3,
        scratch_shapes=[dma((3,))],
        compiler_params=pltpu.CompilerParams(vmem_limit_bytes=63 * 1024 * 1024),
    )(*values)
    return x.reshape(3, X, Y, Z), res.reshape(3, X, Y, Z), tiles.reshape(1, 1, 8, K * K)


def solution(mesh):
    n_gx, n_gy = mesh.shape["gx"], mesh.shape["gy"]
    return jax.shard_map(
        functools.partial(per_device, n_gx, n_gy),
        mesh=mesh,
        in_specs=(P(None, "gx", "gy", None), P("gx", "gy", None), P(None, None, "gx", "gy", None)),
        out_specs=(P(None, "gx", "gy", None), P(None, "gx", "gy", None), P("gx", "gy", None, None)),
        check_vma=False,
    )
```
